256 devices in a mesh: grp: 8 (over y, core), dp: 32 (over z, x).
Axes of the slice: x: 4, y: 4, z: 8, core: 2. Of those that a mesh axis runs over, the one named last changes fastest.
Arguments:
- query: bfloat16 [4096, 64, 576], P(('grp', 'dp')), parts along dimension 0, may hold values from -34 to 34
- cache: bfloat16 [4096, 256, 576], P(('grp', 'dp')), parts along dimension 0, may hold values from -6 to 6
- new_latent: bfloat16 [4096, 576], P(('grp', 'dp')), parts along dimension 0, may hold values from -6 to 6
- lengths: int32 [4096], P(('grp', 'dp')), parts along dimension 0, may hold values from 64 to 256, as said below
- counts: int32 [256], P(('grp', 'dp')), parts along dimension 0, may hold values from 8 to 16, as said below
- hidden_in: bfloat16 [4096, 3584], P(('grp', 'dp')), parts along dimension 0, may hold values from -6 to 6
- value_up: bfloat16 [64, 512, 128], P('dp'), may hold values from -0.75 to 0.75
- out_proj: bfloat16 [8192, 3584], P('dp'), may hold values from -0.0625 to 0.0625
- norm_gain: bfloat16 [3584], replicated, may hold values from 0.099609375 to 1.8984375
- w_gate: bfloat16 [3584, 9216], P(None, 'dp'), may hold values from -0.09375 to 0.09375
- w_up: bfloat16 [3584, 9216], P(None, 'dp'), may hold values from -0.09375 to 0.09375
- w_down: bfloat16 [9216, 3584], P('dp'), may hold values from -0.125 to 0.125
Outputs:
- mixed: bfloat16 [4096, 3584], P(('grp', 'dp')), parts along dimension 0
The draws below stay inside these ranges and needn't reach their ends.
There are 8 independent parts, one for each index of `grp`. The reference program is written for one: setup_inputs(seed, part) draws one part's arguments, and reference() takes and returns one part's arrays. A program takes and returns all parts, laid end to end along the dimension named above; an argument that names none is the same for every part. Nothing has to cross between parts.
Inputs may be any that keep to these rules, and one draw needn't show every extreme that they name: `lengths`: device d holds requests d * 16 to (d + 1) * 16 - 1; some request has exactly 256 cached positions. Slots 0 to counts[d] - 1 of device d are live; some device is full.
All inputs are finite; a program needn't handle non-finite values.
Results may differ from the reference program's by a relative error of at most 0.03.
Values may be sent and summed in bfloat16 or wider, within the bound.
A program may use at most 128 MiB of HBM per device.

```python
import jax
import jax.numpy as jnp
from jax import lax

D = 3584
H = 64
KVL = 512
VHD = 128
FF = 9216
REQ_DEV = 16
CTX = 256
QKD = 576
REQS = 512
N_DP = 32


def latent_base(key):
    return jnp.clip(jax.random.normal(key, (REQS, CTX, QKD), jnp.float32), -6.0, 6.0)


def draw_cache(key, part):
    base_rows = latent_base(key)
    return base_rows.astype(jnp.bfloat16)


def draw_query(key, part):
    key = jax.random.fold_in(key, 5)
    drawn = jnp.clip(jax.random.normal(key, (REQS, H, QKD), jnp.float32), -6.0, 6.0)
    return drawn.astype(jnp.bfloat16)


def draw_lengths(key, part):
    key = jax.random.fold_in(key, 7)
    base_key = jax.random.fold_in(key, 1)
    dev_key = jax.random.fold_in(key, 2)
    top_key = jax.random.fold_in(key, 3)
    base_len = jax.random.randint(base_key, (REQS,), 0, CTX * 3 // 4 + 1)
    dev_factor = jax.random.randint(dev_key, (N_DP, 1), 1, 5)
    dev_factor = jnp.broadcast_to(dev_factor, (N_DP, REQ_DEV)).reshape(REQS)
    result = CTX // 4 + base_len * dev_factor // 4
    longest = jax.random.randint(top_key, (), 0, REQS)
    return result.at[longest].set(CTX).astype(jnp.int32)


def draw_counts(key, part):
    key = jax.random.fold_in(key, 9)
    full_key = jax.random.fold_in(key, 1)
    result = jax.random.randint(key, (N_DP,), REQ_DEV // 2, REQ_DEV + 1)
    fullest = jax.random.randint(full_key, (), 0, N_DP)
    return result.at[fullest].set(REQ_DEV).astype(jnp.int32)


def block_levels(rng, shape, cuts, low, largest):
    def one(dim, parts):
        heights = jax.random.uniform(jax.random.fold_in(jax.random.fold_in(rng, 6), dim), (parts,), jnp.float32, low / len(cuts), largest / len(cuts))
        return jnp.repeat(jnp.exp(heights), shape[dim] // parts).reshape((-1,) + (1,) * (len(shape) - dim - 1))

    loudness = one(*cuts[0])
    for cut in cuts[1:]:
        loudness = loudness * one(*cut)
    return loudness


def gaussian(rng, extent, spread, bound, cuts=(), kind=jnp.bfloat16):
    gain = block_levels(rng, extent, cuts, -0.22, 0.18) if cuts else 1.0
    entries = jax.random.normal(rng, extent, jnp.float32) * spread * gain
    return jnp.minimum(jnp.maximum(entries, -bound), bound).astype(kind)


def setup_inputs(seed: int = 0, part: int = 0) -> dict:
    splits = jax.random.split(jax.random.key(seed), 13)
    part_keys = jax.random.split(jax.random.fold_in(splits[12], part), 13)
    query = draw_query(jax.random.fold_in(jax.random.fold_in(splits[12], part), 71), part)
    cache = draw_cache(jax.random.fold_in(jax.random.fold_in(splits[12], part), 71), part)
    new_latent = gaussian(part_keys[2], (REQS, QKD), 1.0, 6.0, ((0, 32),))
    lengths = draw_lengths(jax.random.fold_in(jax.random.fold_in(splits[12], part), 71), part)
    counts = draw_counts(jax.random.fold_in(jax.random.fold_in(splits[12], part), 71), part)
    hidden_in = gaussian(part_keys[5], (REQS, D), 1.0, 6.0, ((0, 32),))
    value_up = gaussian(splits[6], (H, KVL, VHD), (KVL // 8) ** -0.5, 0.75, ((0, 32),))
    out_proj = gaussian(splits[7], (H * VHD, D), (H * VHD) ** -0.5, 0.0625, ((0, 32),))
    norm_gain = jnp.clip(1.0 + 0.18 * jax.random.normal(splits[8], (D,), jnp.float32), 0.099609375, 1.8984375).astype(jnp.bfloat16)
    w_gate = gaussian(splits[9], (D, FF), D ** -0.5, 0.09375, ((1, 32),))
    w_up = gaussian(splits[10], (D, FF), D ** -0.5, 0.09375, ((1, 32),))
    w_down = gaussian(splits[11], (FF, D), (FF // 4) ** -0.5, 0.125, ((0, 32),))
    return {"query": query, "cache": cache, "new_latent": new_latent, "lengths": lengths, "counts": counts, "hidden_in": hidden_in, "value_up": value_up, "out_proj": out_proj, "norm_gain": norm_gain, "w_gate": w_gate, "w_up": w_up, "w_down": w_down}


score_scale = 192.0 ** (-0.5)

def rms_rows(residual, norm_gain):
    mean_sq = lax.optimization_barrier(jnp.mean(residual * residual, axis=-1, keepdims=True))
    return (residual * lax.rsqrt(mean_sq + 1e-06) * norm_gain.astype(jnp.float32)).astype(jnp.bfloat16)

def reference(query, cache, new_latent, lengths, counts, hidden_in, value_up, out_proj, norm_gain, w_gate, w_up, w_down):
    query32 = query.astype(jnp.float32)
    cache32 = cache.astype(jnp.float32)
    new32 = new_latent.astype(jnp.float32)
    scores = jnp.einsum('rhk,rck->rhc', query32, cache32) * score_scale
    self_score = jnp.einsum('rhk,rk->rh', query32, new32) * score_scale
    positions = jnp.arange(CTX, dtype=jnp.int32)
    in_range = positions[None, None, :] < lengths[:, None, None]
    scores = jnp.where(in_range, scores, -jnp.inf)
    row_max = jnp.maximum(lax.optimization_barrier(jnp.max(scores, axis=-1)), self_score)
    weights = jnp.exp(scores - row_max[..., None])
    self_weight = jnp.exp(self_score - row_max)
    denom_sum = lax.optimization_barrier(jnp.sum(weights, axis=-1)) + self_weight
    weights_b = weights.astype(jnp.bfloat16).astype(jnp.float32)
    self_b = self_weight.astype(jnp.bfloat16).astype(jnp.float32)
    mixed_sum = jnp.einsum('rhc,rcl->rhl', weights_b, cache32[:, :, :KVL]) + self_b[..., None] * new32[:, None, :KVL]
    latent_out = (mixed_sum / denom_sum[..., None]).astype(jnp.bfloat16)
    heads_out = jnp.einsum('rhl,hlv->rhv', latent_out.astype(jnp.float32), value_up.astype(jnp.float32)).astype(jnp.bfloat16)
    flat_heads = heads_out.reshape(REQS, H * VHD)
    residual = hidden_in.astype(jnp.float32) + jnp.dot(flat_heads, out_proj, preferred_element_type=jnp.float32)
    normed = rms_rows(residual, norm_gain)
    gate_act = jnp.dot(normed, w_gate, preferred_element_type=jnp.float32)
    up_act = jnp.dot(normed, w_up, preferred_element_type=jnp.float32)
    inner_act = (jax.nn.silu(gate_act) * up_act).astype(jnp.bfloat16)
    ffn_out = jnp.dot(inner_act, w_down, preferred_element_type=jnp.float32)
    live_rows = (jnp.arange(REQ_DEV, dtype=jnp.int32)[None, :] < counts[:, None]).reshape(REQS)
    return jnp.where(live_rows[:, None], residual + ffn_out, 0.0).astype(jnp.bfloat16)
```

```python
import jax
import jax.numpy as jnp
from jax import lax
from jax.experimental import pallas as pl
from jax.experimental.pallas import tpu as pltpu
from jax.sharding import PartitionSpec as P

score_scale = 192.0 ** (-0.5)
MESH = pl.DeviceIdType.MESH
F32 = jnp.float32
BF16 = jnp.bfloat16

NZ, NX = 8, 4
RB = 16
D = 3584
CA = 1792
CB = D - CA
HA, HB = CA // 2, CB // 2
PLUS, MINUS = 0, 1
RS_ORDER = (4, -3, 3, -2, 2, -1, 1, 0)


def acols(h):
    return slice(h * HA, (h + 1) * HA)


def bcols(h):
    return slice(CA + h * HB, CA + (h + 1) * HB)


class Net:
    def __init__(self):
        self.g = lax.axis_index("grp")
        d = lax.axis_index("dp")
        self.z = d // NX
        self.x = lax.rem(d, NX)

    def zc(self, k):
        return lax.rem(self.z + (k + NZ), NZ)

    def xc(self, k):
        return lax.rem(self.x + (k + NX), NX)

    def zdev(self, k):
        return (self.g, self.zc(k) * NX + self.x)

    def xdev(self, k):
        return (self.g, self.z * NX + self.xc(k))


class Sender:
    def __init__(self):
        self.started = []

    def start(self, src, dst, ssem, rsem, dev):
        copy = pltpu.make_async_remote_copy(
            src_ref=src,
            dst_ref=dst,
            send_sem=ssem,
            recv_sem=rsem,
            device_id=dev,
            device_id_type=MESH,
        )
        copy.start()
        self.started.append(copy)

    def finish(self):
        for copy in self.started:
            copy.wait_send()


def wait_recv(dst, ssem, rsem, dev):
    pltpu.make_async_remote_copy(
        src_ref=dst,
        dst_ref=dst,
        send_sem=ssem,
        recv_sem=rsem,
        device_id=dev,
        device_id_type=MESH,
    ).wait_recv()


RS_SCRATCH = [
    pltpu.VMEM((NZ, NX, RB, D), BF16),
    pltpu.VMEM((3, NZ, RB, CA), BF16),
    pltpu.VMEM((2, 4, 2, RB, HA), BF16),
    pltpu.VMEM((2, 4, 2, NX, RB, HB), BF16),
    pltpu.VMEM((3, RB, CB), BF16),
    pltpu.SemaphoreType.DMA((2, 3, NZ)),
    pltpu.SemaphoreType.DMA((2, 2, 4, 2)),
    pltpu.SemaphoreType.DMA((2, 2, 4, 2)),
    pltpu.SemaphoreType.DMA((2, 3)),
]
N_RS = len(RS_SCRATCH)


def reduce_scatter(net, send, make_part, total, scratch):
    part, ax, az, bz, bx, ax_sem, az_sem, bz_sem, bx_sem = scratch
    z, x = net.z, net.x

    def along_z(k, h, src, buf, sem, add):
        if k == 4:
            d = PLUS if h == 0 else MINUS
            hops = 4
        else:
            d = PLUS if k > 0 else MINUS
            hops = abs(k)
            if hops < 3 or h == d:
                slot = buf.at[d, hops, h]
                wait_recv(slot, sem.at[0, d, hops, h], sem.at[1, d, hops, h], net.zdev(0))
                add(slot)
            else:
                add(None)
        send.start(
            src,
            buf.at[d, hops - 1, h],
            sem.at[0, d, hops - 1, h],
            sem.at[1, d, hops - 1, h],
            net.zdev(1 if d == PLUS else -1),
        )

    def last_z(h, buf, sem):
        for d in (PLUS, MINUS):
            wait_recv(buf.at[d, 0, h], sem.at[0, d, 0, h], sem.at[1, d, 0, h], net.zdev(0))
        return buf[PLUS, 0, h].astype(F32) + buf[MINUS, 0, h].astype(F32)

    def first(i):
        k = RS_ORDER[i]
        c = net.zc(k)
        make_part(c, part)
        for h in range(2):
            cols = bcols(h)
            if k == 0:
                part[c, :, :, cols] = (part[c, :, :, cols].astype(F32) + last_z(h, bz, bz_sem)).astype(BF16)
                continue

            def add(slot):
                if slot is not None:
                    part[c, :, :, cols] = (
                        part[c, :, :, cols].astype(F32) + slot[...].astype(F32)
                    ).astype(BF16)

            along_z(k, h, part.at[c, :, :, cols], bz, bz_sem, add)
        for o in (1, 3, 2):
            send.start(
                part.at[c, net.xc(o), :, 0:CA],
                ax.at[o - 1, i],
                ax_sem.at[0, o - 1, i],
                ax_sem.at[1, o - 1, i],
                net.xdev(o),
            )
        if k == 0:
            for o in (1, 3, 2):
                send.start(
                    part.at[c, net.xc(o), :, CA:D],
                    bx.at[o - 1],
                    bx_sem.at[0, o - 1],
                    bx_sem.at[1, o - 1],
                    net.xdev(o),
                )

    def second(i):
        k = RS_ORDER[i]
        c = net.zc(k)
        for o in (1, 3, 2):
            wait_recv(ax.at[o - 1, i], ax_sem.at[0, o - 1, i], ax_sem.at[1, o - 1, i], net.zdev(0))
        for h in range(2):
            cols = acols(h)
            acc = part[c, x, :, cols].astype(F32)
            for o in range(3):
                acc = acc + ax[o, i, :, cols].astype(F32)
            if k == 0:
                total[:, cols] += acc + last_z(h, az, az_sem)
                continue

            def add(slot):
                value = acc if slot is None else acc + slot[...].astype(F32)
                part[c, x, :, cols] = value.astype(BF16)

            if k == 4:
                add(None)
            along_z(k, h, part.at[c, x, :, cols], az, az_sem, add)

    for i in range(NZ):
        first(i)
        if i:
            second(i - 1)
    second(NZ - 1)
    for o in (1, 3, 2):
        wait_recv(bx.at[o - 1], bx_sem.at[0, o - 1], bx_sem.at[1, o - 1], net.zdev(0))
    acc = part[z, x, :, CA:D].astype(F32)
    for o in range(3):
        acc = acc + bx[o].astype(F32)
    total[:, CA:D] += acc


AG_SCRATCH = [
    pltpu.VMEM((NZ, NX, RB, D), BF16),
    pltpu.SemaphoreType.DMA((2, 3, NZ)),
    pltpu.SemaphoreType.DMA((2, 2, 4)),
    pltpu.SemaphoreType.DMA((2, 2, 4, 2)),
    pltpu.SemaphoreType.DMA((2, 3)),
]
N_AG = len(AG_SCRATCH)


def all_gather(net, send, use, scratch):
    rows, ax_sem, az_sem, bz_sem, bx_sem = scratch
    z, x = net.z, net.x
    step = (1, -1)

    def to_x(i, k):
        c = net.zc(k)
        for o in (1, 3, 2):
            ref = rows.at[c, x, :, 0:CA]
            send.start(ref, ref, ax_sem.at[0, o - 1, i], ax_sem.at[1, o - 1, i], net.xdev(o))

    def from_x(i, k):
        c = net.zc(k)
        for o in (1, 3, 2):
            ref = rows.at[c, net.xc(-o), :, 0:CA]
            wait_recv(ref, ax_sem.at[0, o - 1, i], ax_sem.at[1, o - 1, i], net.zdev(0))

    def a_ref(k, hops, d):
        cols = slice(0, CA) if hops < 4 else acols(d)
        return rows.at[net.zc(k), x, :, cols]

    def a_send(hops, d):
        ref = a_ref(-step[d] * (hops - 1), hops, d)
        sems = az_sem.at[0, d, hops - 1], az_sem.at[1, d, hops - 1]
        send.start(ref, ref, *sems, net.zdev(step[d]))

    def a_wait(hops, d):
        ref = a_ref(-step[d] * hops, hops, d)
        wait_recv(ref, az_sem.at[0, d, hops - 1], az_sem.at[1, d, hops - 1], net.zdev(0))

    def b_send(hops, d, h):
        ref = rows.at[net.zc(-step[d] * (hops - 1)), :, :, bcols(h)]
        sems = bz_sem.at[0, d, hops - 1, h], bz_sem.at[1, d, hops - 1, h]
        send.start(ref, ref, *sems, net.zdev(step[d]))

    def b_wait(hops, d, h):
        ref = rows.at[net.zc(-step[d] * hops), :, :, bcols(h)]
        sems = bz_sem.at[0, d, hops - 1, h], bz_sem.at[1, d, hops - 1, h]
        wait_recv(ref, *sems, net.zdev(0))

    own_b = rows.at[z, x, :, CA:D]
    for o in (1, 3, 2):
        send.start(own_b, own_b, bx_sem.at[0, o - 1], bx_sem.at[1, o - 1], net.xdev(o))
    for d in (PLUS, MINUS):
        a_send(1, d)
    to_x(0, 0)
    for o in (1, 3, 2):
        ref = rows.at[z, net.xc(-o), :, CA:D]
        wait_recv(ref, bx_sem.at[0, o - 1], bx_sem.at[1, o - 1], net.zdev(0))
    for h in range(2):
        for d in (PLUS, MINUS):
            b_send(1, d, h if d == PLUS else 1 - h)
    pending = [(0, 0)]

    def use_next():
        i, k = pending.pop(0)
        from_x(i, k)
        use(net.zc(k))

    i = 1
    for hops in range(1, 4):
        for d in (PLUS, MINUS):
            k = -step[d] * hops
            a_wait(hops, d)
            a_send(hops + 1, d)
            to_x(i, k)
            for h in (d, 1 - d):
                b_wait(hops, d, h)
                if hops < 3 or h == d:
                    b_send(hops + 1, d, h)
            use_next()
            pending.append((i, k))
            i += 1
    for d in (PLUS, MINUS):
        a_wait(4, d)
    to_x(i, 4)
    pending.append((i, 4))
    use_next()
    for d in (PLUS, MINUS):
        b_wait(4, d, d)
    while pending:
        use_next()


def block_kernel(
    heads,
    hidden,
    gain,
    counts,
    wo_hbm,
    wg_hbm,
    wu_hbm,
    wd_hbm,
    out,
    wo,
    wg,
    wu,
    wd,
    w_sem,
    inner,
    total,
    ffn,
    *scratch,
):
    rs1, rs2, ag = scratch[:N_RS], scratch[N_RS : 2 * N_RS], scratch[2 * N_RS :]
    net = Net()
    send = Sender()
    weights = [
        pltpu.make_async_copy(src, dst, w_sem.at[i])
        for i, (src, dst) in enumerate(((wo_hbm, wo), (wg_hbm, wg), (wu_hbm, wu), (wd_hbm, wd)))
    ]
    for copy in weights:
        copy.start()
    barrier = pltpu.get_barrier_semaphore()
    partners = [net.zdev(1), net.zdev(-1)] + [net.xdev(o) for o in (1, 2, 3)]
    for dev in partners:
        pl.semaphore_signal(barrier, inc=1, device_id=dev, device_id_type=MESH)
    pl.semaphore_wait(barrier, len(partners))

    weights[0].wait()

    def project(c, part):
        value = jnp.dot(heads[c], wo[...], preferred_element_type=F32)
        part[c] = value.astype(BF16).reshape(NX, RB, D)

    total[...] = hidden[...].astype(F32)
    reduce_scatter(net, send, project, total, rs1)

    rows = ag[0]
    residual = total[...]
    mean_sq = jnp.mean(residual * residual, axis=-1, keepdims=True)
    rows[net.z, net.x] = (residual * lax.rsqrt(mean_sq + 1e-06) * gain[...].astype(F32)).astype(BF16)

    weights[1].wait()
    weights[2].wait()

    def feed(c):
        chunk = rows[c].reshape(NX * RB, D)
        gate = jnp.dot(chunk, wg[...], preferred_element_type=F32)
        up = jnp.dot(chunk, wu[...], preferred_element_type=F32)
        inner[c] = (gate / (1.0 + jnp.exp(-gate)) * up).astype(BF16)

    all_gather(net, send, feed, ag)

    weights[3].wait()

    def down(c, part):
        value = jnp.dot(inner[c], wd[...], preferred_element_type=F32)
        part[c] = value.astype(BF16).reshape(NX, RB, D)

    ffn[...] = total[...]
    reduce_scatter(net, send, down, ffn, rs2)
    live = lax.broadcasted_iota(jnp.int32, (RB, D), 0) < counts[0]
    out[...] = jnp.where(live, ffn[...], 0.0).astype(BF16)
    send.finish()


def block(heads, hidden, gain, counts, wo, wg, wu, wd):
    vmem = pl.BlockSpec(memory_space=pltpu.VMEM)
    hbm = pl.BlockSpec(memory_space=pl.ANY)
    n_inner = wg.shape[1]
    return pl.pallas_call(
        block_kernel,
        out_shape=jax.ShapeDtypeStruct((RB, D), BF16),
        in_specs=[vmem, vmem, vmem, pl.BlockSpec(memory_space=pltpu.SMEM), hbm, hbm, hbm, hbm],
        out_specs=vmem,
        scratch_shapes=[
            pltpu.VMEM(wo.shape, BF16),
            pltpu.VMEM(wg.shape, BF16),
            pltpu.VMEM(wu.shape, BF16),
            pltpu.VMEM(wd.shape, BF16),
            pltpu.SemaphoreType.DMA((4,)),
            pltpu.VMEM((NZ, NX * RB, n_inner), BF16),
            pltpu.VMEM((RB, D), F32),
            pltpu.VMEM((RB, D), F32),
            *RS_SCRATCH,
            *RS_SCRATCH,
            *AG_SCRATCH,
        ],
        compiler_params=pltpu.CompilerParams(
            collective_id=1, has_side_effects=True, vmem_limit_bytes=56 << 20
        ),
        name="block",
    )(heads, hidden, gain, counts, wo, wg, wu, wd)


def per_device(
    query,
    cache,
    new_latent,
    lengths,
    counts,
    hidden_in,
    value_up,
    out_proj,
    norm_gain,
    w_gate,
    w_up,
    w_down,
):
    latent_width = value_up.shape[1]
    scores = (
        jnp.einsum("rhk,rck->rhc", query, cache, preferred_element_type=jnp.float32) * score_scale
    )
    self_score = (
        jnp.einsum("rhk,rk->rh", query, new_latent, preferred_element_type=jnp.float32)
        * score_scale
    )
    positions = jnp.arange(cache.shape[1], dtype=jnp.int32)
    in_range = positions[None, None, :] < lengths[:, None, None]
    scores = jnp.where(in_range, scores, -jnp.inf)
    row_max = jnp.maximum(jnp.max(scores, axis=-1), self_score)
    weights = jnp.exp(scores - row_max[..., None])
    self_weight = jnp.exp(self_score - row_max)
    denom_sum = jnp.sum(weights, axis=-1) + self_weight
    weights_b = weights.astype(jnp.bfloat16)
    self_b = self_weight.astype(jnp.bfloat16).astype(jnp.float32)
    mixed_sum = jnp.einsum(
        "rhc,rcl->rhl", weights_b, cache[:, :, :latent_width], preferred_element_type=jnp.float32
    )
    mixed_sum = mixed_sum + self_b[..., None] * new_latent[:, None, :latent_width].astype(
        jnp.float32
    )
    latent_out = (mixed_sum / denom_sum[..., None]).astype(jnp.bfloat16)
    exchanged = lax.all_to_all(latent_out, "dp", split_axis=1, concat_axis=0, tiled=True)
    heads_out = jnp.einsum(
        "rhl,hlv->rhv", exchanged, value_up, preferred_element_type=jnp.float32
    ).astype(jnp.bfloat16)
    heads = heads_out.reshape(NZ, NX * RB, -1)
    return block(
        heads, hidden_in, norm_gain.reshape(1, D), counts, out_proj, w_gate, w_up, w_down
    )


def solution(mesh):
    return jax.shard_map(
        per_device,
        mesh=mesh,
        in_specs=(
            P(("grp", "dp"), None, None),
            P(("grp", "dp"), None, None),
            P(("grp", "dp"), None),
            P(("grp", "dp")),
            P(("grp", "dp")),
            P(("grp", "dp"), None),
            P("dp", None, None),
            P("dp", None),
            P(),
            P(None, "dp"),
            P(None, "dp"),
            P("dp", None),
        ),
        out_specs=P(("grp", "dp"), None),
        check_vma=False,
    )
```

```python
import jax
import jax.numpy as jnp
from jax import lax
from jax.experimental import pallas as pl
from jax.experimental.pallas import tpu as pltpu
from jax.sharding import PartitionSpec as P

score_scale = 192.0 ** (-0.5)
MESH = pl.DeviceIdType.MESH
F32 = jnp.float32
BF16 = jnp.bfloat16

NZ, NX = 8, 4
RB = 16
D = 3584
KVL = 512
VHD = 128
CTX = 256
CA = 1792
CB = D - CA
HA, HB = CA // 2, CB // 2
PLUS, MINUS = 0, 1
RS_ORDER = (4, -3, 3, -2, 2, -1, 1, 0)


def acols(h):
    return slice(h * HA, (h + 1) * HA)


def bcols(h):
    return slice(CA + h * HB, CA + (h + 1) * HB)


class Net:
    def __init__(self):
        self.g = lax.axis_index("grp")
        d = lax.axis_index("dp")
        self.z = d // NX
        self.x = lax.rem(d, NX)

    def zc(self, k):
        return lax.rem(self.z + (k + NZ), NZ)

    def xc(self, k):
        return lax.rem(self.x + (k + NX), NX)

    def zdev(self, k):
        return (self.g, self.zc(k) * NX + self.x)

    def xdev(self, k):
        return (self.g, self.z * NX + self.xc(k))


class Sender:
    def __init__(self):
        self.started = []

    def start(self, src, dst, ssem, rsem, dev):
        copy = pltpu.make_async_remote_copy(
            src_ref=src,
            dst_ref=dst,
            send_sem=ssem,
            recv_sem=rsem,
            device_id=dev,
            device_id_type=MESH,
        )
        copy.start()
        self.started.append(copy)

    def finish(self):
        for copy in self.started:
            copy.wait_send()


def wait_recv(dst, ssem, rsem, dev):
    pltpu.make_async_remote_copy(
        src_ref=dst,
        dst_ref=dst,
        send_sem=ssem,
        recv_sem=rsem,
        device_id=dev,
        device_id_type=MESH,
    ).wait_recv()


RS_SCRATCH = [
    pltpu.VMEM((NZ, NX, RB, D), BF16),
    pltpu.VMEM((3, NZ, RB, CA), BF16),
    pltpu.VMEM((2, 4, 2, RB, HA), BF16),
    pltpu.VMEM((2, 4, 2, NX, RB, HB), BF16),
    pltpu.VMEM((3, RB, CB), BF16),
    pltpu.SemaphoreType.DMA((2, 3, NZ)),
    pltpu.SemaphoreType.DMA((2, 2, 4, 2)),
    pltpu.SemaphoreType.DMA((2, 2, 4, 2)),
    pltpu.SemaphoreType.DMA((2, 3)),
]
N_RS = len(RS_SCRATCH)


def reduce_scatter(net, send, make_part, total, scratch):
    part, ax, az, bz, bx, ax_sem, az_sem, bz_sem, bx_sem = scratch
    z, x = net.z, net.x

    def along_z(k, h, src, buf, sem, add):
        if k == 4:
            d = PLUS if h == 0 else MINUS
            hops = 4
        else:
            d = PLUS if k > 0 else MINUS
            hops = abs(k)
            if hops < 3 or h == d:
                slot = buf.at[d, hops, h]
                wait_recv(slot, sem.at[0, d, hops, h], sem.at[1, d, hops, h], net.zdev(0))
                add(slot)
            else:
                add(None)
        send.start(
            src,
            buf.at[d, hops - 1, h],
            sem.at[0, d, hops - 1, h],
            sem.at[1, d, hops - 1, h],
            net.zdev(1 if d == PLUS else -1),
        )

    def last_z(h, buf, sem):
        for d in (PLUS, MINUS):
            wait_recv(buf.at[d, 0, h], sem.at[0, d, 0, h], sem.at[1, d, 0, h], net.zdev(0))
        return buf[PLUS, 0, h].astype(F32) + buf[MINUS, 0, h].astype(F32)

    def first(i):
        k = RS_ORDER[i]
        c = net.zc(k)
        make_part(k, c, part)
        for h in range(2):
            cols = bcols(h)
            if k == 0:
                part[c, :, :, cols] = (part[c, :, :, cols].astype(F32) + last_z(h, bz, bz_sem)).astype(BF16)
                continue

            def add(slot):
                if slot is not None:
                    part[c, :, :, cols] = (
                        part[c, :, :, cols].astype(F32) + slot[...].astype(F32)
                    ).astype(BF16)

            along_z(k, h, part.at[c, :, :, cols], bz, bz_sem, add)
        for o in (1, 3, 2):
            send.start(
                part.at[c, net.xc(o), :, 0:CA],
                ax.at[o - 1, i],
                ax_sem.at[0, o - 1, i],
                ax_sem.at[1, o - 1, i],
                net.xdev(o),
            )
        if k == 0:
            for o in (1, 3, 2):
                send.start(
                    part.at[c, net.xc(o), :, CA:D],
                    bx.at[o - 1],
                    bx_sem.at[0, o - 1],
                    bx_sem.at[1, o - 1],
                    net.xdev(o),
                )

    def second(i):
        k = RS_ORDER[i]
        c = net.zc(k)
        for o in (1, 3, 2):
            wait_recv(ax.at[o - 1, i], ax_sem.at[0, o - 1, i], ax_sem.at[1, o - 1, i], net.zdev(0))
        for h in range(2):
            cols = acols(h)
            acc = part[c, x, :, cols].astype(F32)
            for o in range(3):
                acc = acc + ax[o, i, :, cols].astype(F32)
            if k == 0:
                total[:, cols] += acc + last_z(h, az, az_sem)
                continue

            def add(slot):
                value = acc if slot is None else acc + slot[...].astype(F32)
                part[c, x, :, cols] = value.astype(BF16)

            if k == 4:
                add(None)
            along_z(k, h, part.at[c, x, :, cols], az, az_sem, add)

    for i in range(NZ):
        first(i)
        if i:
            second(i - 1)
    second(NZ - 1)
    for o in (1, 3, 2):
        wait_recv(bx.at[o - 1], bx_sem.at[0, o - 1], bx_sem.at[1, o - 1], net.zdev(0))
    acc = part[z, x, :, CA:D].astype(F32)
    for o in range(3):
        acc = acc + bx[o].astype(F32)
    total[:, CA:D] += acc


AG_SCRATCH = [
    pltpu.VMEM((NZ, NX, RB, D), BF16),
    pltpu.SemaphoreType.DMA((2, 3, NZ)),
    pltpu.SemaphoreType.DMA((2, 2, 4)),
    pltpu.SemaphoreType.DMA((2, 2, 4, 2)),
    pltpu.SemaphoreType.DMA((2, 3)),
]
N_AG = len(AG_SCRATCH)


def all_gather(net, send, use, scratch):
    rows, ax_sem, az_sem, bz_sem, bx_sem = scratch
    z, x = net.z, net.x
    step = (1, -1)

    def to_x(i, k):
        c = net.zc(k)
        for o in (1, 3, 2):
            ref = rows.at[c, x, :, 0:CA]
            send.start(ref, ref, ax_sem.at[0, o - 1, i], ax_sem.at[1, o - 1, i], net.xdev(o))

    def from_x(i, k):
        c = net.zc(k)
        for o in (1, 3, 2):
            ref = rows.at[c, net.xc(-o), :, 0:CA]
            wait_recv(ref, ax_sem.at[0, o - 1, i], ax_sem.at[1, o - 1, i], net.zdev(0))

    def a_ref(k, hops, d):
        cols = slice(0, CA) if hops < 4 else acols(d)
        return rows.at[net.zc(k), x, :, cols]

    def a_send(hops, d):
        ref = a_ref(-step[d] * (hops - 1), hops, d)
        sems = az_sem.at[0, d, hops - 1], az_sem.at[1, d, hops - 1]
        send.start(ref, ref, *sems, net.zdev(step[d]))

    def a_wait(hops, d):
        ref = a_ref(-step[d] * hops, hops, d)
        wait_recv(ref, az_sem.at[0, d, hops - 1], az_sem.at[1, d, hops - 1], net.zdev(0))

    def b_send(hops, d, h):
        ref = rows.at[net.zc(-step[d] * (hops - 1)), :, :, bcols(h)]
        sems = bz_sem.at[0, d, hops - 1, h], bz_sem.at[1, d, hops - 1, h]
        send.start(ref, ref, *sems, net.zdev(step[d]))

    def b_wait(hops, d, h):
        ref = rows.at[net.zc(-step[d] * hops), :, :, bcols(h)]
        sems = bz_sem.at[0, d, hops - 1, h], bz_sem.at[1, d, hops - 1, h]
        wait_recv(ref, *sems, net.zdev(0))

    own_b = rows.at[z, x, :, CA:D]
    for o in (1, 3, 2):
        send.start(own_b, own_b, bx_sem.at[0, o - 1], bx_sem.at[1, o - 1], net.xdev(o))
    for d in (PLUS, MINUS):
        a_send(1, d)
    to_x(0, 0)
    for o in (1, 3, 2):
        ref = rows.at[z, net.xc(-o), :, CA:D]
        wait_recv(ref, bx_sem.at[0, o - 1], bx_sem.at[1, o - 1], net.zdev(0))
    for h in range(2):
        for d in (PLUS, MINUS):
            b_send(1, d, h if d == PLUS else 1 - h)
    pending = [(0, 0)]

    def use_next():
        i, k = pending.pop(0)
        from_x(i, k)
        use(net.zc(k))

    i = 1
    for hops in range(1, 4):
        for d in (PLUS, MINUS):
            k = -step[d] * hops
            a_wait(hops, d)
            a_send(hops + 1, d)
            to_x(i, k)
            for h in (d, 1 - d):
                b_wait(hops, d, h)
                if hops < 3 or h == d:
                    b_send(hops + 1, d, h)
            use_next()
            pending.append((i, k))
            i += 1
    for d in (PLUS, MINUS):
        a_wait(4, d)
    to_x(i, 4)
    pending.append((i, 4))
    use_next()
    for d in (PLUS, MINUS):
        b_wait(4, d, d)
    while pending:
        use_next()


class Inbox:
    def __init__(self, send, sems, home):
        self.send, self.sems, self.home = send, sems, home

    def push(self, src, dst, index, dev):
        self.send.start(src, dst, self.sems.at[(0, *index)], self.sems.at[(1, *index)], dev)

    def wait(self, dst, index):
        wait_recv(dst, self.sems.at[(0, *index)], self.sems.at[(1, *index)], self.home)


class ValueUp:
    def __init__(self, net, send, vu, z_sem, core_sem):
        self.net, self.vu = net, vu
        self.core = lax.rem(net.g, 2)
        self.other = (net.g + 1 - 2 * self.core, net.z * NX + net.x)
        home = net.zdev(0)
        self.along = Inbox(send, z_sem, home)
        self.across = Inbox(send, core_sem, home)

    def ref(self, k, hops, d, head):
        rows = slice(0, KVL) if hops < 4 else slice(d * (KVL // 2), (d + 1) * (KVL // 2))
        return self.vu.at[self.net.zc(k), head, rows]

    def start(self, hops):
        for d, step in ((PLUS, 1), (MINUS, -1)):
            ref = self.ref(-step * (hops - 1), hops, d, self.core)
            self.along.push(ref, ref, (d, hops - 1), self.net.zdev(step))

    def forward(self, hops):
        for d, step in ((PLUS, 1), (MINUS, -1)):
            ref = self.ref(-step * hops, hops, d, self.core)
            self.along.wait(ref, (d, hops - 1))
            self.across.push(ref, ref, (d, hops - 1), self.other)
        if hops < 4:
            self.start(hops + 1)

    def finish(self):
        for hops in range(1, 5):
            for d, step in ((PLUS, 1), (MINUS, -1)):
                self.across.wait(self.ref(-step * hops, hops, d, 1 - self.core), (d, hops - 1))


def order_matrix(n, source):
    i = lax.broadcasted_iota(jnp.int32, (n, n), 0)
    j = lax.broadcasted_iota(jnp.int32, (n, n), 1)
    return jnp.where(source(i) == j, 1.0, 0.0).astype(BF16)


def attend(rs, query, cache, new_latent, lengths, order, lat):
    qs = [query[r] for r in rs]
    scores = [jnp.dot(q, cache[r], preferred_element_type=F32) * score_scale for q, r in zip(qs, rs)]
    news = [new_latent[r : r + 1, :].astype(F32) for r in rs]
    own = [
        jnp.sum(q.astype(F32) * new, axis=-1, keepdims=True) * score_scale
        for q, new in zip(qs, news)
    ]
    position = lax.broadcasted_iota(jnp.int32, (1, CTX), 1)
    scores = [jnp.where(position < lengths[r], s, -jnp.inf) for s, r in zip(scores, rs)]
    tops = [jnp.maximum(jnp.max(s, axis=-1, keepdims=True), o) for s, o in zip(scores, own)]
    weights = [jnp.exp(s - top) for s, top in zip(scores, tops)]
    own = [jnp.exp(o - top) for o, top in zip(own, tops)]
    sums = [jnp.sum(w, axis=-1, keepdims=True) + o for w, o in zip(weights, own)]
    mixed = [
        lax.dot_general(
            w.astype(BF16),
            cache[r, 0:KVL, :],
            (((1,), (1,)), ((), ())),
            preferred_element_type=F32,
        )
        for w, r in zip(weights, rs)
    ]
    latent = [
        ((m + o.astype(BF16).astype(F32) * new[:, 0:KVL]) * (1.0 / s)).astype(BF16)
        for m, o, new, s in zip(mixed, own, news, sums)
    ]
    latent = [jnp.dot(order, value, preferred_element_type=F32).astype(BF16) for value in latent]
    for value, r in zip(latent, rs):
        for to in range(NX):
            lat[to, r] = value[to * 16 : (to + 1) * 16]


GROUPS = 4
SIZE = RB // GROUPS


def layer_kernel(
    query_hbm,
    cache_hbm,
    new_latent,
    lengths,
    vu_hbm,
    hidden,
    gain,
    counts,
    wo_hbm,
    wg_hbm,
    wu_hbm,
    wd_hbm,
    out,
    query,
    cache,
    vu,
    lat,
    lat_in,
    by_head,
    heads_out,
    heads,
    q_sem,
    c_sem,
    v_sem,
    lat_sem,
    heads_sem,
    vz_sem,
    vcore_sem,
    wo,
    wg,
    wu,
    wd,
    w_sem,
    inner,
    total,
    ffn,
    *scratch,
):
    rs1, rs2, ag = scratch[:N_RS], scratch[N_RS : 2 * N_RS], scratch[2 * N_RS :]
    net = Net()
    z, x = net.z, net.x
    home = net.zdev(0)
    send = Sender()

    loads = []
    for i in range(GROUPS):
        part = pl.ds(i * SIZE, SIZE)
        loads.append(
            (
                pltpu.make_async_copy(query_hbm.at[part], query.at[part], q_sem.at[i]),
                pltpu.make_async_copy(cache_hbm.at[part], cache.at[part], c_sem.at[i]),
            )
        )
    own_vu = pltpu.make_async_copy(vu_hbm, vu.at[z], v_sem.at[0])
    weights = [
        pltpu.make_async_copy(src, dst, w_sem.at[i])
        for i, (src, dst) in enumerate(((wo_hbm, wo), (wg_hbm, wg), (wu_hbm, wu), (wd_hbm, wd)))
    ]
    for copy in [own_vu, *loads[0], *loads[1], *loads[2], *loads[3], *weights]:
        copy.start()

    value_up = ValueUp(net, send, vu, vz_sem, vcore_sem)
    z_others = (4, -3, 3, -2, 2, -1, 1)
    barrier = pltpu.get_barrier_semaphore()
    partners = [net.zdev(k) for k in z_others] + [net.xdev(o) for o in (1, 2, 3)] + [value_up.other]
    for dev in partners:
        pl.semaphore_signal(barrier, inc=1, device_id=dev, device_id_type=MESH)
    pl.semaphore_wait(barrier, len(partners))

    own_vu.wait()
    value_up.start(1)

    order = order_matrix(
        64, lambda i: ((i & 15) >> 1) * 8 + (i >> 4) * 2 + (i & 1)
    )
    lat_box = Inbox(send, lat_sem, home)
    for i in range(GROUPS):
        for copy in loads[i]:
            copy.wait()
        attend(range(i * SIZE, (i + 1) * SIZE), query, cache, new_latent, lengths, order, lat)
        part = pl.ds(i * SIZE, SIZE)
        for o in (1, 3, 2):
            lat_box.push(lat.at[net.xc(o), part], lat_in.at[o - 1, part], (o - 1, i), net.xdev(o))
        if i % 2:
            value_up.forward(i // 2 + 1)

    swap = order_matrix(256, lambda i: ((i & 15) << 4) + (i >> 4))

    def sort(o):
        rows = lat[x] if o == 0 else lat_in[o - 1]
        value = jnp.dot(swap, rows.reshape(RB * 16, KVL), preferred_element_type=F32)
        by_head[:, net.xc(-o)] = value.astype(BF16).reshape(16, RB, KVL)

    sort(0)
    value_up.forward(3)
    for o in (1, 3, 2):
        for i in range(GROUPS):
            lat_box.wait(lat_in.at[o - 1, pl.ds(i * SIZE, SIZE)], (o - 1, i))
        sort(o)
    value_up.forward(4)
    value_up.finish()

    heads_box = Inbox(send, heads_sem, home)
    for i, k in enumerate((*z_others, 0)):
        c = net.zc(k)
        target = heads if k == 0 else heads_out
        for j in range(2):
            rows = by_head[c * 2 + j].reshape(NX * RB, KVL)
            value = jnp.dot(rows, vu[c, j], preferred_element_type=F32)
            target[c, :, j * VHD : (j + 1) * VHD] = value.astype(BF16)
        if k:
            heads_box.push(heads_out.at[c], heads.at[z], (i,), net.zdev(k))

    weights[0].wait()

    def project(k, c, part):
        if k:
            heads_box.wait(heads.at[c], (z_others.index(-k if k < 4 else 4),))
        value = jnp.dot(heads[c], wo[...], preferred_element_type=F32)
        part[c] = value.astype(BF16).reshape(NX, RB, D)

    total[...] = hidden[...].astype(F32)
    reduce_scatter(net, send, project, total, rs1)

    rows = ag[0]
    residual = total[...]
    mean_sq = jnp.mean(residual * residual, axis=-1, keepdims=True)
    rows[z, x] = (residual * lax.rsqrt(mean_sq + 1e-06) * gain[...].astype(F32)).astype(BF16)

    weights[1].wait()
    weights[2].wait()

    def feed(c):
        chunk = rows[c].reshape(NX * RB, D)
        dims = (((1,), (1,)), ((), ()))
        gate = lax.dot_general(chunk, wg[...], dims, preferred_element_type=F32)
        up = lax.dot_general(chunk, wu[...], dims, preferred_element_type=F32)
        inner[c] = (gate / (1.0 + jnp.exp(-gate)) * up).astype(BF16)

    all_gather(net, send, feed, ag)

    weights[3].wait()

    def down(k, c, part):
        value = jnp.dot(inner[c], wd[...], preferred_element_type=F32)
        part[c] = value.astype(BF16).reshape(NX, RB, D)

    ffn[...] = total[...]
    reduce_scatter(net, send, down, ffn, rs2)
    live = lax.broadcasted_iota(jnp.int32, (RB, D), 0) < counts[0]
    out[...] = jnp.where(live, ffn[...], 0.0).astype(BF16)
    send.finish()


def per_device(
    query,
    cache,
    new_latent,
    lengths,
    counts,
    hidden_in,
    value_up,
    out_proj,
    norm_gain,
    w_gate,
    w_up,
    w_down,
):
    cache = cache.transpose(0, 2, 1)
    w_gate, w_up = w_gate.T, w_up.T
    vmem = pl.BlockSpec(memory_space=pltpu.VMEM)
    smem = pl.BlockSpec(memory_space=pltpu.SMEM)
    hbm = pl.BlockSpec(memory_space=pl.ANY)
    return pl.pallas_call(
        layer_kernel,
        out_shape=jax.ShapeDtypeStruct((RB, D), BF16),
        in_specs=[hbm, hbm, vmem, smem, hbm, vmem, vmem, smem, hbm, hbm, hbm, hbm],
        out_specs=vmem,
        scratch_shapes=[
            pltpu.VMEM(query.shape, BF16),
            pltpu.VMEM(cache.shape, BF16),
            pltpu.VMEM((NZ, 2, KVL, VHD), BF16),
            pltpu.VMEM((NX, RB, 16, KVL), BF16),
            pltpu.VMEM((3, RB, 16, KVL), BF16),
            pltpu.VMEM((16, NX, RB, KVL), BF16),
            pltpu.VMEM((NZ, NX * RB, 2 * VHD), BF16),
            pltpu.VMEM((NZ, NX * RB, 2 * VHD), BF16),
            pltpu.SemaphoreType.DMA((GROUPS,)),
            pltpu.SemaphoreType.DMA((GROUPS,)),
            pltpu.SemaphoreType.DMA((1,)),
            pltpu.SemaphoreType.DMA((2, 3, GROUPS)),
            pltpu.SemaphoreType.DMA((2, 7)),
            pltpu.SemaphoreType.DMA((2, 2, 4)),
            pltpu.SemaphoreType.DMA((2, 2, 4)),
            pltpu.VMEM(out_proj.shape, BF16),
            pltpu.VMEM(w_gate.shape, BF16),
            pltpu.VMEM(w_up.shape, BF16),
            pltpu.VMEM(w_down.shape, BF16),
            pltpu.SemaphoreType.DMA((4,)),
            pltpu.VMEM((NZ, NX * RB, w_gate.shape[0]), BF16),
            pltpu.VMEM((RB, D), F32),
            pltpu.VMEM((RB, D), F32),
            *RS_SCRATCH,
            *RS_SCRATCH,
            *AG_SCRATCH,
        ],
        compiler_params=pltpu.CompilerParams(
            collective_id=1, has_side_effects=True, vmem_limit_bytes=60 << 20
        ),
        name="layer",
    )(
        query,
        cache,
        new_latent,
        lengths,
        value_up,
        hidden_in,
        norm_gain.reshape(1, D),
        counts,
        out_proj,
        w_gate,
        w_up,
        w_down,
    )


def solution(mesh):
    return jax.shard_map(
        per_device,
        mesh=mesh,
        in_specs=(
            P(("grp", "dp"), None, None),
            P(("grp", "dp"), None, None),
            P(("grp", "dp"), None),
            P(("grp", "dp")),
            P(("grp", "dp")),
            P(("grp", "dp"), None),
            P("dp", None, None),
            P("dp", None),
            P(),
            P(None, "dp"),
            P(None, "dp"),
            P("dp", None),
        ),
        out_specs=P(("grp", "dp"), None),
        check_vma=False,
    )
```

```python
import jax
import jax.numpy as jnp
from jax import lax
from jax.experimental import pallas as pl
from jax.experimental.pallas import tpu as pltpu
from jax.sharding import PartitionSpec as P

score_scale = 192.0 ** (-0.5)
MESH = pl.DeviceIdType.MESH
F32 = jnp.float32
BF16 = jnp.bfloat16

NZ, NX, NY = 8, 4, 4
RB = 16
ZB = NX * RB
D = 3584
DX = D // NX
KVL = 512
VHD = 128
CTX = 256
FD = 288
FM, FR, FREP = 256, 32, 4
FK = FM + FR * FREP
CA = 384
PLUS, MINUS = 0, 1
TREE_A, TREE_H, TREE_I = False, False, False
EARLY = False
FAR = True
STEP = (1, -1)
XO = (1, 3, 2)
RS_ORDER = (4, -3, 3, -2, 2, -1, 1, 0)


def half(h):
    return slice(h * ZB // 2, (h + 1) * ZB // 2)


class Net:
    def __init__(self):
        self.g = lax.axis_index("grp")
        self.d = lax.axis_index("dp")
        self.z = self.d // NX
        self.x = lax.rem(self.d, NX)
        self.y = self.g // 2
        self.core = lax.rem(self.g, 2)
        self.sibling = (self.g + 1 - 2 * self.core, self.d)

    def zc(self, k):
        return lax.rem(self.z + (k + NZ), NZ)

    def xc(self, k):
        return lax.rem(self.x + (k + NX), NX)

    def yc(self, k):
        return lax.rem(self.y + (k + NY), NY)

    def zdev(self, k):
        return (self.g, self.zc(k) * NX + self.x)

    def xdev(self, k):
        return (self.g, self.z * NX + self.xc(k))

    def ydev(self, k):
        return (self.yc(k) * 2 + self.core, self.d)


def xcols(q):
    if isinstance(q, int):
        return slice(q * DX, (q + 1) * DX)
    return pl.ds(pl.multiple_of(q * DX, 128), DX)


class Sender:
    def __init__(self):
        self.started = []

    def start(self, src, dst, ssem, rsem, dev):
        copy = pltpu.make_async_remote_copy(
            src_ref=src,
            dst_ref=dst,
            send_sem=ssem,
            recv_sem=rsem,
            device_id=dev,
            device_id_type=MESH,
        )
        copy.start()
        self.started.append(copy)

    def finish(self):
        for copy in self.started:
            copy.wait_send()


def wait_recv(dst, ssem, rsem, dev):
    pltpu.make_async_remote_copy(
        src_ref=dst,
        dst_ref=dst,
        send_sem=ssem,
        recv_sem=rsem,
        device_id=dev,
        device_id_type=MESH,
    ).wait_recv()


class Inbox:
    def __init__(self, send, sems, home):
        self.send, self.sems, self.home = send, sems, home

    def push(self, src, dst, index, dev):
        self.send.start(src, dst, self.sems.at[(0, *index)], self.sems.at[(1, *index)], dev)

    def wait(self, dst, index):
        wait_recv(dst, self.sems.at[(0, *index)], self.sems.at[(1, *index)], self.home)


class AlongX:
    def __init__(self, net, send, block, sem, tree):
        self.net, self.block = net, block
        self.box = Inbox(send, sem, net.zdev(0))
        self.tree = tree

    def relayed(self, k):
        return self.tree and k != 4

    def push(self, k):
        i = RS_ORDER.index(k)
        ref = self.block(k, self.net.x, None)
        for d in (PLUS, MINUS):
            self.box.push(ref, ref, (i, d, 0), self.net.xdev(STEP[d]))
        if not self.relayed(k):
            self.box.push(ref, ref, (i, 0, 1), self.net.xdev(2))

    def relay(self, k, last=False):
        if not (self.relayed(k) or last):
            return
        i = RS_ORDER.index(k)
        for d in (PLUS, MINUS):
            come = self.net.xc(-STEP[d])
            self.box.wait(self.block(k, come, None), (i, d, 0))
            if not last:
                ref = self.block(k, come, d)
                self.box.push(ref, ref, (i, d, 1), self.net.xdev(STEP[d]))

    def finish(self, k):
        i = RS_ORDER.index(k)
        if not self.relayed(k):
            self.relay(k, True)
            self.box.wait(self.block(k, self.net.xc(2), None), (i, 0, 1))
            return
        for d in (PLUS, MINUS):
            self.box.wait(self.block(k, self.net.xc(2), d), (i, d, 1))


ALONG_X_SEM = pltpu.SemaphoreType.DMA((2, NZ, 2, 2))


class Regroup:
    def __init__(self, net, send, own, buf, x_sem, y_sem, core_sem):
        self.net, self.own, self.buf = net, own, buf
        home = net.zdev(0)
        self.over_x = Inbox(send, x_sem, home)
        self.over_y = Inbox(send, y_sem, home)
        self.across = Inbox(send, core_sem, home)

    def start(self):
        net = self.net
        for o in XO:
            src = self.own.at[:, xcols(net.xc(o))]
            self.over_x.push(src, self.buf.at[net.x, net.g], (o - 1,), net.xdev(o))
        self.buf[net.x, net.g] = self.own[:, xcols(net.x)]

    def spread(self):
        net = self.net
        for o in XO:
            self.over_x.wait(self.buf.at[net.xc(-o), net.g], (o - 1,))
        ref = self.buf.at[:, net.g]
        for o in XO:
            self.over_y.push(ref, ref, (o - 1,), net.ydev(o))
        self.across.push(ref, ref, (0,), net.sibling)

    def pass_on(self):
        net = self.net
        for o in XO:
            ref = self.buf.at[:, net.yc(-o) * 2 + net.core]
            self.over_y.wait(ref, (o - 1,))
            self.across.push(ref, ref, (o,), net.sibling)

    def finish(self):
        net = self.net
        for o in range(NY):
            self.across.wait(self.buf.at[:, net.yc(-o) * 2 + 1 - net.core], (o,))


REGROUP_SEMS = [
    pltpu.SemaphoreType.DMA((2, 3)),
    pltpu.SemaphoreType.DMA((2, 3)),
    pltpu.SemaphoreType.DMA((2, 4)),
]

SUM_SCRATCH = [
    pltpu.VMEM((NZ, ZB, DX), BF16),
    pltpu.VMEM((2, 4, 2, ZB // 2, DX), BF16),
    pltpu.SemaphoreType.DMA((2, 2, 4, 2)),
]


class SumZ:
    def __init__(self, net, send, part, came, sem):
        self.net, self.part, self.came = net, part, came
        self.box = Inbox(send, sem, net.zdev(0))

    def step(self, k, term, chained=True):
        c = self.net.zc(k)
        d = PLUS if k > 0 else MINUS
        for h in (0, 1) if k == 4 else (1 - d, d):
            value = term[half(h)]
            hops = abs(k)
            if k == 4:
                d = h
            elif hops < 3 or (chained and h == d):
                self.box.wait(self.came.at[d, hops, h], (d, hops, h))
                value = value + self.came[d, hops, h].astype(F32)
            self.part[c, half(h)] = value.astype(BF16)
            self.box.push(
                self.part.at[c, half(h)],
                self.came.at[d, hops - 1, h],
                (d, hops - 1, h),
                self.net.zdev(STEP[d]),
            )

    def last(self, h):
        for d in (PLUS, MINUS):
            self.box.wait(self.came.at[d, 0, h], (d, 0, h))
        return self.came[PLUS, 0, h].astype(F32) + self.came[MINUS, 0, h].astype(F32)


AG_SCRATCH = [
    pltpu.VMEM((NZ, NX, ZB, DX), BF16),
    ALONG_X_SEM,
    pltpu.SemaphoreType.DMA((2, 2, 4)),
    pltpu.SemaphoreType.DMA((2, 2, 4, 2)),
    pltpu.SemaphoreType.DMA((2, 3)),
]


def all_gather(net, send, use, between, rows, ax_sem, az_sem, bz_sem, bx_sem):
    z, x = net.z, net.x
    home = net.zdev(0)
    az, bz, bx = (Inbox(send, sem, home) for sem in (az_sem, bz_sem, bx_sem))

    def a_block(k, q, h):
        return rows.at[net.zc(k), q, slice(0, ZB) if h is None else half(h), 0:CA]

    ax = AlongX(net, send, a_block, ax_sem, TREE_A)

    def a_ref(k, hops, d):
        return rows.at[net.zc(k), x, slice(0, ZB) if hops < 4 else half(d), 0:CA]

    def a_send(hops, d):
        ref = a_ref(-STEP[d] * (hops - 1), hops, d)
        az.push(ref, ref, (d, hops - 1), net.zdev(STEP[d]))

    def b_ref(k, h):
        return rows.at[net.zc(k), :, half(h), CA:DX]

    def b_send(hops, d, h):
        ref = b_ref(-STEP[d] * (hops - 1), h)
        bz.push(ref, ref, (d, hops - 1, h), net.zdev(STEP[d]))

    def step_a(hops):
        for d in (PLUS, MINUS):
            az.wait(a_ref(-STEP[d] * hops, hops, d), (d, hops - 1))
            if hops < 4:
                a_send(hops + 1, d)
                ax.push(-STEP[d] * hops)
        if hops == 4:
            ax.push(4)

    def step_b(hops, far):
        for d in (PLUS, MINUS):
            h = d if far else 1 - d
            bz.wait(b_ref(-STEP[d] * hops, h), (d, hops - 1, h))
            if hops < 3 or (hops == 3 and far):
                b_send(hops + 1, d, h)

    def finish(k):
        ax.finish(k)
        use(k)

    for d in (PLUS, MINUS):
        a_send(1, d)
    own_b = rows.at[z, x, :, CA:DX]
    for o in XO:
        bx.push(own_b, own_b, (o - 1,), net.xdev(o))
    ax.push(0)
    step_a(1)
    for o in XO:
        bx.wait(rows.at[z, net.xc(-o), :, CA:DX], (o - 1,))
    for far in (True, False):
        for d in (PLUS, MINUS):
            b_send(1, d, d if far else 1 - d)
    ax.relay(0)
    step_a(2)
    ax.relay(-1)
    ax.relay(1)
    finish(0)
    step_b(1, True)
    step_a(3)
    ax.relay(-2)
    ax.relay(2)
    step_b(1, False)
    step_a(4)
    finish(-1)
    ax.relay(-3)
    ax.relay(3)
    finish(1)
    step_b(2, True)
    ax.relay(4)
    step_b(2, False)
    finish(-2)
    step_b(3, True)
    finish(2)
    step_b(3, False)
    between(0)
    finish(-3)
    finish(3)
    step_b(4, True)
    between(1)
    finish(4)


class ValueUp:
    def __init__(self, net, send, vu, z_sem, core_sem):
        self.net, self.vu = net, vu
        self.core, self.other = net.core, net.sibling
        home = net.zdev(0)
        self.along = Inbox(send, z_sem, home)
        self.across = Inbox(send, core_sem, home)

    def ref(self, k, hops, d, head):
        rows = slice(0, KVL) if hops < 4 else slice(d * (KVL // 2), (d + 1) * (KVL // 2))
        return self.vu.at[self.net.zc(k), head, rows]

    def start(self, hops):
        for d, step in ((PLUS, 1), (MINUS, -1)):
            ref = self.ref(-step * (hops - 1), hops, d, self.core)
            self.along.push(ref, ref, (d, hops - 1), self.net.zdev(step))

    def forward(self, hops):
        for d, step in ((PLUS, 1), (MINUS, -1)):
            ref = self.ref(-step * hops, hops, d, self.core)
            self.along.wait(ref, (d, hops - 1))
            self.across.push(ref, ref, (d, hops - 1), self.other)
        if hops < 4:
            self.start(hops + 1)

    def finish(self):
        for hops in range(1, 5):
            for d, step in ((PLUS, 1), (MINUS, -1)):
                self.across.wait(self.ref(-step * hops, hops, d, 1 - self.core), (d, hops - 1))


def order_matrix(n, source):
    i = lax.broadcasted_iota(jnp.int32, (n, n), 0)
    j = lax.broadcasted_iota(jnp.int32, (n, n), 1)
    return jnp.where(source(i) == j, 1.0, 0.0).astype(BF16)


def attend(rs, query, cache, new_latent, lengths, order, lat):
    qs = [query[r] for r in rs]
    scores = [jnp.dot(q, cache[r], preferred_element_type=F32) * score_scale for q, r in zip(qs, rs)]
    news = [new_latent[r : r + 1, :].astype(F32) for r in rs]
    own = [
        jnp.sum(q.astype(F32) * new, axis=-1, keepdims=True) * score_scale
        for q, new in zip(qs, news)
    ]
    position = lax.broadcasted_iota(jnp.int32, (1, CTX), 1)
    scores = [jnp.where(position < lengths[r], s, -jnp.inf) for s, r in zip(scores, rs)]
    tops = [jnp.maximum(jnp.max(s, axis=-1, keepdims=True), o) for s, o in zip(scores, own)]
    weights = [jnp.exp(s - top) for s, top in zip(scores, tops)]
    own = [jnp.exp(o - top) for o, top in zip(own, tops)]
    sums = [jnp.sum(w, axis=-1, keepdims=True) + o for w, o in zip(weights, own)]
    mixed = [
        lax.dot_general(
            w.astype(BF16),
            cache[r, 0:KVL, :],
            (((1,), (1,)), ((), ())),
            preferred_element_type=F32,
        )
        for w, r in zip(weights, rs)
    ]
    latent = [
        ((m + o.astype(BF16).astype(F32) * new[:, 0:KVL]) * (1.0 / s)).astype(BF16)
        for m, o, new, s in zip(mixed, own, news, sums)
    ]
    latent = [jnp.dot(order, value, preferred_element_type=F32).astype(BF16) for value in latent]
    for value, r in zip(latent, rs):
        for to in range(NX):
            lat[to, r] = value[to * 16 : (to + 1) * 16]


GROUPS = 4
SIZE = RB // GROUPS


def layer_kernel(
    query_hbm,
    cache_hbm,
    new_latent,
    lengths,
    vu_hbm,
    hidden,
    gain,
    counts,
    wo_hbm,
    wg_hbm,
    wu_hbm,
    wd_hbm,
    out,
    query,
    cache,
    vu,
    lat,
    lat_in,
    by_head,
    heads_out,
    heads,
    q_sem,
    c_sem,
    lat_sem,
    heads_sem,
    heads_x_sem,
    vz_sem,
    vcore_sem,
    wo_own,
    wo,
    wd_own,
    wd_in,
    wd,
    wg,
    wu,
    own_sem,
    w_sem,
    inner,
    inner_sem,
    hid,
    hid_sem,
    square,
    square_in,
    square_sem,
    total,
    result,
    result_in,
    result_sem,
    far,
    far_in,
    far_sem,
    *scratch,
):
    net = Net()
    z, x = net.z, net.x
    home = net.zdev(0)
    send = Sender()
    sum_heads = SumZ(net, send, *scratch[0:3])
    sum_ffn = SumZ(net, send, *scratch[3:6])
    wo_group = Regroup(net, send, wo_own, wo, *scratch[6:9])
    wd_group = Regroup(net, send, wd_own, wd_in, *scratch[9:12])
    ag = scratch[12:]

    z_others = RS_ORDER[:-1]
    barrier = pltpu.get_barrier_semaphore()
    partners = [net.zdev(k) for k in z_others] + [net.xdev(o) for o in XO]
    partners += [net.ydev(o) for o in XO] + [net.sibling]
    for dev in partners:
        pl.semaphore_signal(barrier, inc=1, device_id=dev, device_id_type=MESH)

    loads = []
    for i in range(GROUPS):
        part = pl.ds(i * SIZE, SIZE)
        loads.append(
            (
                pltpu.make_async_copy(query_hbm.at[part], query.at[part], q_sem.at[i]),
                pltpu.make_async_copy(cache_hbm.at[part], cache.at[part], c_sem.at[i]),
            )
        )
    own_vu = pltpu.make_async_copy(vu_hbm, vu.at[z], own_sem.at[0])
    own_wo = pltpu.make_async_copy(
        wo_hbm.at[pl.ds(pl.multiple_of(net.g * 32, 32), 32)], wo_own, own_sem.at[1]
    )
    own_wd = pltpu.make_async_copy(
        wd_hbm.at[pl.ds(pl.multiple_of(net.y * 64 + net.core * 48, 16), 48)], wd_own, own_sem.at[2]
    )
    weights = []
    for i, (src, dst) in enumerate(((wg_hbm, wg), (wu_hbm, wu))):
        weights.append(pltpu.make_async_copy(src, dst.at[0:FD], w_sem.at[i, 0]))
        for j in range(1, FREP):
            weights.append(
                pltpu.make_async_copy(
                    src.at[FM:FD], dst.at[FM + j * FR : FM + (j + 1) * FR], w_sem.at[i, j]
                )
            )

    def begin(copies):
        for copy in copies:
            copy.start()

    begin([*loads[0], own_vu, own_wo, *loads[1]])

    value_up = ValueUp(net, send, vu, vz_sem, vcore_sem)
    order = order_matrix(
        64, lambda i: ((i & 15) >> 1) * 8 + (i >> 4) * 2 + (i & 1)
    )
    lat_box = Inbox(send, lat_sem, home)
    hid_box = Inbox(send, hid_sem, home)
    later = ([*loads[2]], [*loads[3]], [own_wd], weights)
    for i in range(GROUPS):
        for copy in loads[i]:
            copy.wait()
        begin(later[i])
        attend(range(i * SIZE, (i + 1) * SIZE), query, cache, new_latent, lengths, order, lat)
        if i == 0:
            own_vu.wait()
            own_wo.wait()
            pl.semaphore_wait(barrier, len(partners))
            value_up.start(1)
            wo_group.start()
        part = pl.ds(i * SIZE, SIZE)
        for o in XO:
            lat_box.push(lat.at[net.xc(o), part], lat_in.at[o - 1, part], (o - 1, i), net.xdev(o))
        if i == 1:
            wo_group.spread()
            value_up.forward(1)
    for o in XO:
        hid_box.push(hidden.at[:, xcols(net.xc(o))], hid.at[x], (o - 1,), net.xdev(o))
    hid[x] = hidden[:, xcols(x)]
    value_up.forward(2)

    swap = order_matrix(256, lambda i: ((i & 15) << 4) + (i >> 4))

    def sort(o):
        rows = lat[x] if o == 0 else lat_in[o - 1]
        value = jnp.dot(swap, rows.reshape(RB * 16, KVL), preferred_element_type=F32)
        by_head[:, net.xc(-o)] = value.astype(BF16).reshape(16, RB, KVL)

    sort(0)
    value_up.forward(3)
    wo_group.pass_on()
    for o in XO:
        for i in range(GROUPS):
            lat_box.wait(lat_in.at[o - 1, pl.ds(i * SIZE, SIZE)], (o - 1, i))
        sort(o)
    own_wd.wait()
    wd_group.start()
    value_up.forward(4)
    value_up.finish()

    heads_box = Inbox(send, heads_sem, home)
    for i, k in enumerate(RS_ORDER):
        c = net.zc(k)
        for j in range(2):
            rows = by_head[c * 2 + j].reshape(ZB, KVL)
            value = jnp.dot(rows, vu[c, j], preferred_element_type=F32).astype(BF16)
            cols = slice(j * VHD, (j + 1) * VHD)
            if k:
                heads_out[c, :, cols] = value
            else:
                heads[z, x, :, cols] = value
        if k:
            heads_box.push(heads_out.at[c], heads.at[z, x], (i,), net.zdev(k))

    def heads_block(k, q, h):
        return heads.at[net.zc(k), q, slice(0, ZB) if h is None else half(h)]

    heads_x = AlongX(net, send, heads_block, heads_x_sem, TREE_H)

    def project(k):
        c = net.zc(k)
        heads_x.finish(k)
        rows = jnp.concatenate([heads[c, q] for q in range(NX)], axis=1)
        term = jnp.dot(rows, wo[...].reshape(NX * 256, DX), preferred_element_type=F32)
        if k:
            sum_heads.step(k, term)
            return
        for o in XO:
            hid_box.wait(hid.at[net.xc(-o)], (o - 1,))
        for h in range(2):
            before = hid[2 * h : 2 * h + 2].reshape(ZB // 2, DX).astype(F32)
            total[half(h)] = before + (term[half(h)] + sum_heads.last(h))

    for i, k in enumerate(RS_ORDER):
        if k:
            heads_box.wait(heads.at[net.zc(k), x], (z_others.index(-k if k < 4 else 4),))
        heads_x.push(k)
        if i == 2 and EARLY:
            wo_group.finish()
        if i:
            heads_x.relay(RS_ORDER[i - 1])
        if i > 2 and EARLY:
            project(RS_ORDER[i - 3])
    if not EARLY:
        wo_group.finish()
    wd_group.spread()
    heads_x.relay(0)
    for k in RS_ORDER[5 if EARLY else 0 :]:
        project(k)

    rows = ag[0]
    residual = total[...]
    sums = jnp.sum(residual * residual, axis=-1, keepdims=True)
    square[...] = jnp.broadcast_to(sums, (ZB, 128))
    square_box = Inbox(send, square_sem, home)
    for o in XO:
        square_box.push(square, square_in.at[o - 1], (o - 1,), net.xdev(o))
    for o in XO:
        square_box.wait(square_in.at[o - 1], (o - 1,))
        sums = sums + square_in[o - 1][:, 0:1]
    mean_sq = sums * (1.0 / D)
    scaled = total[...] * lax.rsqrt(mean_sq + 1e-06) * gain[:, xcols(x)].astype(F32)
    rows[z, x] = scaled.astype(BF16)

    for copy in weights:
        copy.wait()

    def inner_block(k, q, h):
        part = (slice(0, 80), slice(80, 2 * ZB + RB))[h] if h is not None else slice(0, 2 * ZB + RB)
        return inner.at[net.zc(k), q, part]

    inner_x = AlongX(net, send, inner_block, inner_sem, TREE_I)
    fed = []
    lane = lax.broadcasted_iota(jnp.int32, (RB, FR * FREP), 1) // FR

    def feed(k):
        c = net.zc(k)
        chunk = jnp.concatenate([rows[c, q] for q in range(NX)], axis=1)
        dims = (((1,), (1,)), ((), ()))
        gate = lax.dot_general(chunk, wg[...], dims, preferred_element_type=F32)
        up = lax.dot_general(chunk, wu[...], dims, preferred_element_type=F32)
        act = gate / (1.0 + jnp.exp(-gate)) * up
        for j in range(2):
            inner[c, x, j * ZB : (j + 1) * ZB] = act[:, j * 128 : (j + 1) * 128].astype(BF16)
        rest = act[:, FM:FK]
        packed = rest[0:RB]
        for q in range(1, FREP):
            packed = jnp.where(lane == q, rest[q * RB : (q + 1) * RB], packed)
        inner[c, x, 2 * ZB : 2 * ZB + RB] = packed.astype(BF16)
        inner_x.push(k)
        if fed:
            inner_x.relay(fed[-1])
        fed.append(k)

    def between(stage):
        if stage == 0:
            wd_group.pass_on()
            return
        wd_group.finish()
        for q in range(NX):
            for g, low, count, to in (
                (0, 0, 48, 0),
                (1, 0, 48, 48),
                (2, 32, 16, 96),
                (3, 0, 48, 112),
                (4, 32, 16, 160),
                (5, 0, 48, 176),
                (6, 32, 16, 224),
                (7, 0, 16, 240),
            ):
                wd[q * FM + to : q * FM + to + count] = wd_in[q, g, low : low + count]
            for j in range(FREP):
                to = NX * FM + (q * FREP + j) * FR
                wd[to : to + FR] = wd_in[q, 7, 16 : 16 + FR]

    all_gather(net, send, feed, between, *ag)

    far_box = Inbox(send, far_sem, home)
    group = lax.broadcasted_iota(jnp.int32, (ZB, FR * FREP), 1) // FR
    mine = group == lax.broadcasted_iota(jnp.int32, (ZB, FR * FREP), 0) // RB
    for k in (-3, 3, 4, -2, 2, -1, 1, 0) if FAR else RS_ORDER:
        c = net.zc(k)
        inner_x.finish(k)
        columns = []
        for q in range(NX):
            columns += [inner[c, q, 0:ZB], inner[c, q, ZB : 2 * ZB]]
        for q in range(NX):
            rest = jnp.concatenate([inner[c, q, 2 * ZB : 2 * ZB + RB]] * FREP, axis=0)
            columns.append(jnp.where(mine, rest, jnp.zeros_like(rest)))
        term = jnp.dot(jnp.concatenate(columns, axis=1), wd[...], preferred_element_type=F32)
        if k == 4 and FAR:
            far[...] = term.astype(BF16)
            far_box.push(far, far_in, (), net.zdev(4))
            continue
        if k:
            sum_ffn.step(k, term, chained=not FAR)
            continue
        if FAR:
            far_box.wait(far_in, ())
            term = term + far_in[...].astype(F32)
        for h in range(2):
            value = total[half(h)] + (term[half(h)] + sum_ffn.last(h))
            result[2 * h : 2 * h + 2] = value.astype(BF16).reshape(2, RB, DX)

    result_box = Inbox(send, result_sem, home)
    for o in XO:
        result_box.push(result.at[net.xc(o)], result_in.at[x], (o - 1,), net.xdev(o))
    result_in[x] = result[x]
    for o in XO:
        result_box.wait(result_in.at[net.xc(-o)], (o - 1,))
    live = lax.broadcasted_iota(jnp.int32, (RB, DX), 0) < counts[0]
    for q in range(NX):
        value = result_in[q]
        out[:, xcols(q)] = jnp.where(live, value, jnp.zeros_like(value))
    send.finish()


def per_device(
    query,
    cache,
    new_latent,
    lengths,
    counts,
    hidden_in,
    value_up,
    out_proj,
    norm_gain,
    w_gate,
    w_up,
    w_down,
):
    cache = cache.transpose(0, 2, 1)
    w_gate, w_up = w_gate.T, w_up.T
    vmem = pl.BlockSpec(memory_space=pltpu.VMEM)
    smem = pl.BlockSpec(memory_space=pltpu.SMEM)
    hbm = pl.BlockSpec(memory_space=pl.ANY)
    dma = pltpu.SemaphoreType.DMA
    return pl.pallas_call(
        layer_kernel,
        out_shape=jax.ShapeDtypeStruct((RB, D), BF16),
        in_specs=[hbm, hbm, vmem, smem, hbm, vmem, vmem, smem, hbm, hbm, hbm, hbm],
        out_specs=vmem,
        scratch_shapes=[
            pltpu.VMEM(query.shape, BF16),
            pltpu.VMEM(cache.shape, BF16),
            pltpu.VMEM((NZ, 2, KVL, VHD), BF16),
            pltpu.VMEM((NX, RB, 16, KVL), BF16),
            pltpu.VMEM((3, RB, 16, KVL), BF16),
            pltpu.VMEM((16, NX, RB, KVL), BF16),
            pltpu.VMEM((NZ, ZB, 2 * VHD), BF16),
            pltpu.VMEM((NZ, NX, ZB, 2 * VHD), BF16),
            dma((GROUPS,)),
            dma((GROUPS,)),
            dma((2, 3, GROUPS)),
            dma((2, 7)),
            ALONG_X_SEM,
            dma((2, 2, 4)),
            dma((2, 2, 4)),
            pltpu.VMEM((32, D), BF16),
            pltpu.VMEM((NX, 8, 32, DX), BF16),
            pltpu.VMEM((48, D), BF16),
            pltpu.VMEM((NX, 8, 48, DX), BF16),
            pltpu.VMEM((NX * FK, DX), BF16),
            pltpu.VMEM((FK, D), BF16),
            pltpu.VMEM((FK, D), BF16),
            dma((3,)),
            dma((2, FREP)),
            pltpu.VMEM((NZ, NX, 2 * ZB + RB, 128), BF16),
            ALONG_X_SEM,
            pltpu.VMEM((NX, RB, DX), BF16),
            dma((2, 3)),
            pltpu.VMEM((ZB, 128), F32),
            pltpu.VMEM((3, ZB, 128), F32),
            dma((2, 3)),
            pltpu.VMEM((ZB, DX), F32),
            pltpu.VMEM((NX, RB, DX), BF16),
            pltpu.VMEM((NX, RB, DX), BF16),
            dma((2, 3)),
            pltpu.VMEM((ZB, DX), BF16),
            pltpu.VMEM((ZB, DX), BF16),
            dma((2,)),
            *SUM_SCRATCH,
            *SUM_SCRATCH,
            *REGROUP_SEMS,
            *REGROUP_SEMS,
            *AG_SCRATCH,
        ],
        compiler_params=pltpu.CompilerParams(
            collective_id=1, has_side_effects=True, vmem_limit_bytes=60 << 20
        ),
        name="layer",
    )(
        query,
        cache,
        new_latent,
        lengths,
        value_up,
        hidden_in,
        norm_gain.reshape(1, D),
        counts,
        out_proj,
        w_gate,
        w_up,
        w_down,
    )


def solution(mesh):
    return jax.shard_map(
        per_device,
        mesh=mesh,
        in_specs=(
            P(("grp", "dp"), None, None),
            P(("grp", "dp"), None, None),
            P(("grp", "dp"), None),
            P(("grp", "dp")),
            P(("grp", "dp")),
            P(("grp", "dp"), None),
            P("dp", None, None),
            P("dp", None),
            P(),
            P(None, "dp"),
            P(None, "dp"),
            P("dp", None),
        ),
        out_specs=P(("grp", "dp"), None),
        check_vma=False,
    )
```

```python
import jax
import jax.numpy as jnp
from jax import lax
from jax.experimental import pallas as pl
from jax.experimental.pallas import tpu as pltpu
from jax.sharding import PartitionSpec as P

score_scale = 192.0 ** (-0.5)
MESH = pl.DeviceIdType.MESH
F32 = jnp.float32
BF16 = jnp.bfloat16

NZ, NX, NY = 8, 4, 4
RB = 16
ZB = NX * RB
D = 3584
DX = D // NX
KVL = 512
VHD = 128
CTX = 256
FD = 288
FM, FR, FREP = 256, 32, 4
FK = FM + FR * FREP
CA = 384
PLUS, MINUS = 0, 1
STEP = (1, -1)
XO = (1, 3, 2)
RS_ORDER = (4, -3, 3, -2, 2, -1, 1, 0)


def half(h):
    return slice(h * ZB // 2, (h + 1) * ZB // 2)


class Net:
    def __init__(self):
        self.g = lax.axis_index("grp")
        self.d = lax.axis_index("dp")
        self.z = self.d // NX
        self.x = lax.rem(self.d, NX)
        self.y = self.g // 2
        self.core = lax.rem(self.g, 2)
        self.sibling = (self.g + 1 - 2 * self.core, self.d)

    def zc(self, k):
        return lax.rem(self.z + (k + NZ), NZ)

    def xc(self, k):
        return lax.rem(self.x + (k + NX), NX)

    def yc(self, k):
        return lax.rem(self.y + (k + NY), NY)

    def zdev(self, k):
        return (self.g, self.zc(k) * NX + self.x)

    def xdev(self, k):
        return (self.g, self.z * NX + self.xc(k))

    def ydev(self, k):
        return (self.yc(k) * 2 + self.core, self.d)


def xcols(q):
    if isinstance(q, int):
        return slice(q * DX, (q + 1) * DX)
    return pl.ds(pl.multiple_of(q * DX, 128), DX)


class Sender:
    def __init__(self):
        self.started = []

    def start(self, src, dst, ssem, rsem, dev):
        copy = pltpu.make_async_remote_copy(
            src_ref=src,
            dst_ref=dst,
            send_sem=ssem,
            recv_sem=rsem,
            device_id=dev,
            device_id_type=MESH,
        )
        copy.start()
        self.started.append(copy)

    def finish(self):
        for copy in self.started:
            copy.wait_send()


def wait_recv(dst, ssem, rsem, dev):
    pltpu.make_async_remote_copy(
        src_ref=dst,
        dst_ref=dst,
        send_sem=ssem,
        recv_sem=rsem,
        device_id=dev,
        device_id_type=MESH,
    ).wait_recv()


class Inbox:
    def __init__(self, send, sems, home):
        self.send, self.sems, self.home = send, sems, home

    def push(self, src, dst, index, dev):
        self.send.start(src, dst, self.sems.at[(0, *index)], self.sems.at[(1, *index)], dev)

    def wait(self, dst, index):
        wait_recv(dst, self.sems.at[(0, *index)], self.sems.at[(1, *index)], self.home)


class AlongX:
    def __init__(self, net, send, block, sem):
        self.net, self.block = net, block
        self.box = Inbox(send, sem, net.zdev(0))

    def push(self, k):
        ref = self.block(k, self.net.x)
        for o in XO:
            self.box.push(ref, ref, (o - 1, RS_ORDER.index(k)), self.net.xdev(o))

    def finish(self, k):
        for o in XO:
            self.box.wait(self.block(k, self.net.xc(-o)), (o - 1, RS_ORDER.index(k)))


ALONG_X_SEM = pltpu.SemaphoreType.DMA((2, 3, NZ))


class Regroup:
    def __init__(self, net, send, own, buf, x_sem, y_sem, core_sem):
        self.net, self.own, self.buf = net, own, buf
        home = net.zdev(0)
        self.over_x = Inbox(send, x_sem, home)
        self.over_y = Inbox(send, y_sem, home)
        self.across = Inbox(send, core_sem, home)

    def start(self):
        net = self.net
        for o in XO:
            src = self.own.at[:, xcols(net.xc(o))]
            self.over_x.push(src, self.buf.at[net.x, net.g], (o - 1,), net.xdev(o))
        self.buf[net.x, net.g] = self.own[:, xcols(net.x)]

    def spread(self):
        net = self.net
        for o in XO:
            self.over_x.wait(self.buf.at[net.xc(-o), net.g], (o - 1,))
        ref = self.buf.at[:, net.g]
        for o in XO:
            self.over_y.push(ref, ref, (o - 1,), net.ydev(o))
        self.across.push(ref, ref, (0,), net.sibling)

    def pass_on(self):
        net = self.net
        for o in XO:
            ref = self.buf.at[:, net.yc(-o) * 2 + net.core]
            self.over_y.wait(ref, (o - 1,))
            self.across.push(ref, ref, (o,), net.sibling)

    def finish(self):
        net = self.net
        for o in range(NY):
            self.across.wait(self.buf.at[:, net.yc(-o) * 2 + 1 - net.core], (o,))


REGROUP_SEMS = [
    pltpu.SemaphoreType.DMA((2, 3)),
    pltpu.SemaphoreType.DMA((2, 3)),
    pltpu.SemaphoreType.DMA((2, 4)),
]

SUM_SCRATCH = [
    pltpu.VMEM((NZ, ZB, DX), BF16),
    pltpu.VMEM((2, 4, 2, ZB // 2, DX), BF16),
    pltpu.SemaphoreType.DMA((2, 2, 4, 2)),
]


class SumZ:
    def __init__(self, net, send, part, came, sem):
        self.net, self.part, self.came = net, part, came
        self.box = Inbox(send, sem, net.zdev(0))

    def step(self, k, term, chained=True):
        c = self.net.zc(k)
        d = PLUS if k > 0 else MINUS
        for h in (0, 1) if k == 4 else (1 - d, d):
            value = term[half(h)]
            hops = abs(k)
            if k == 4:
                d = h
            elif hops < 3 or (chained and h == d):
                self.box.wait(self.came.at[d, hops, h], (d, hops, h))
                value = value + self.came[d, hops, h].astype(F32)
            self.part[c, half(h)] = value.astype(BF16)
            self.box.push(
                self.part.at[c, half(h)],
                self.came.at[d, hops - 1, h],
                (d, hops - 1, h),
                self.net.zdev(STEP[d]),
            )

    def last(self, h):
        for d in (PLUS, MINUS):
            self.box.wait(self.came.at[d, 0, h], (d, 0, h))
        return self.came[PLUS, 0, h].astype(F32) + self.came[MINUS, 0, h].astype(F32)


AG_SCRATCH = [
    pltpu.VMEM((NZ, NX, ZB, DX), BF16),
    ALONG_X_SEM,
    pltpu.SemaphoreType.DMA((2, 2, 4)),
    pltpu.SemaphoreType.DMA((2, 2, 4, 2)),
    pltpu.SemaphoreType.DMA((2, 3)),
]


def all_gather(net, send, use, between, rows, ax_sem, az_sem, bz_sem, bx_sem):
    z, x = net.z, net.x
    home = net.zdev(0)
    az, bz, bx = (Inbox(send, sem, home) for sem in (az_sem, bz_sem, bx_sem))

    def a_block(k, q):
        return rows.at[net.zc(k), q, :, 0:CA]

    ax = AlongX(net, send, a_block, ax_sem)

    def a_ref(k, hops, d):
        return rows.at[net.zc(k), x, slice(0, ZB) if hops < 4 else half(d), 0:CA]

    def a_send(hops, d):
        ref = a_ref(-STEP[d] * (hops - 1), hops, d)
        az.push(ref, ref, (d, hops - 1), net.zdev(STEP[d]))

    def b_ref(k, h):
        return rows.at[net.zc(k), :, half(h), CA:DX]

    def b_send(hops, d, h):
        ref = b_ref(-STEP[d] * (hops - 1), h)
        bz.push(ref, ref, (d, hops - 1, h), net.zdev(STEP[d]))

    def step_a(hops):
        for d in (PLUS, MINUS):
            az.wait(a_ref(-STEP[d] * hops, hops, d), (d, hops - 1))
            if hops < 4:
                a_send(hops + 1, d)
                ax.push(-STEP[d] * hops)
        if hops == 4:
            ax.push(4)

    def step_b(hops, far):
        for d in (PLUS, MINUS):
            h = d if far else 1 - d
            bz.wait(b_ref(-STEP[d] * hops, h), (d, hops - 1, h))
            if hops < 3 or (hops == 3 and far):
                b_send(hops + 1, d, h)

    def finish(*ks):
        for k in ks:
            ax.finish(k)
        use(ks)

    for d in (PLUS, MINUS):
        a_send(1, d)
    own_b = rows.at[z, x, :, CA:DX]
    for o in XO:
        bx.push(own_b, own_b, (o - 1,), net.xdev(o))
    ax.push(0)
    step_a(1)
    for o in XO:
        bx.wait(rows.at[z, net.xc(-o), :, CA:DX], (o - 1,))
    for far in (True, False):
        for d in (PLUS, MINUS):
            b_send(1, d, d if far else 1 - d)
    step_a(2)
    finish(0)
    step_b(1, True)
    step_a(3)
    step_b(1, False)
    step_a(4)
    finish(-1, 1)
    step_b(2, True)
    step_b(2, False)
    finish(-2, 2)
    step_b(3, True)
    step_b(3, False)
    between(0)
    finish(-3, 3)
    step_b(4, True)
    between(1)
    finish(4)


class ValueUp:
    def __init__(self, net, send, vu, z_sem, core_sem):
        self.net, self.vu = net, vu
        self.core, self.other = net.core, net.sibling
        home = net.zdev(0)
        self.along = Inbox(send, z_sem, home)
        self.across = Inbox(send, core_sem, home)

    def ref(self, k, hops, d, head):
        rows = slice(0, KVL) if hops < 4 else slice(d * (KVL // 2), (d + 1) * (KVL // 2))
        return self.vu.at[self.net.zc(k), head, rows]

    def start(self, hops):
        for d, step in ((PLUS, 1), (MINUS, -1)):
            ref = self.ref(-step * (hops - 1), hops, d, self.core)
            self.along.push(ref, ref, (d, hops - 1), self.net.zdev(step))

    def forward(self, hops):
        for d, step in ((PLUS, 1), (MINUS, -1)):
            ref = self.ref(-step * hops, hops, d, self.core)
            self.along.wait(ref, (d, hops - 1))
            self.across.push(ref, ref, (d, hops - 1), self.other)
        if hops < 4:
            self.start(hops + 1)

    def finish(self):
        for hops in range(1, 5):
            for d, step in ((PLUS, 1), (MINUS, -1)):
                self.across.wait(self.ref(-step * hops, hops, d, 1 - self.core), (d, hops - 1))


def order_matrix(n, source):
    i = lax.broadcasted_iota(jnp.int32, (n, n), 0)
    j = lax.broadcasted_iota(jnp.int32, (n, n), 1)
    return jnp.where(source(i) == j, 1.0, 0.0).astype(BF16)


def attend(rs, query, cache, new_latent, lengths, order, lat):
    qs = [query[r] for r in rs]
    scores = [jnp.dot(q, cache[r], preferred_element_type=F32) * score_scale for q, r in zip(qs, rs)]
    news = [new_latent[r : r + 1, :].astype(F32) for r in rs]
    own = [
        jnp.sum(q.astype(F32) * new, axis=-1, keepdims=True) * score_scale
        for q, new in zip(qs, news)
    ]
    position = lax.broadcasted_iota(jnp.int32, (1, CTX), 1)
    scores = [jnp.where(position < lengths[r], s, -jnp.inf) for s, r in zip(scores, rs)]
    tops = [jnp.maximum(jnp.max(s, axis=-1, keepdims=True), o) for s, o in zip(scores, own)]
    weights = [jnp.exp(s - top) for s, top in zip(scores, tops)]
    own = [jnp.exp(o - top) for o, top in zip(own, tops)]
    sums = [jnp.sum(w, axis=-1, keepdims=True) + o for w, o in zip(weights, own)]
    mixed = [
        lax.dot_general(
            w.astype(BF16),
            cache[r, 0:KVL, :],
            (((1,), (1,)), ((), ())),
            preferred_element_type=F32,
        )
        for w, r in zip(weights, rs)
    ]
    latent = [
        ((m + o.astype(BF16).astype(F32) * new[:, 0:KVL]) * (1.0 / s)).astype(BF16)
        for m, o, new, s in zip(mixed, own, news, sums)
    ]
    latent = [jnp.dot(order, value, preferred_element_type=F32).astype(BF16) for value in latent]
    for value, r in zip(latent, rs):
        for to in range(NX):
            lat[to, r] = value[to * 16 : (to + 1) * 16]


GROUPS = 4
SIZE = RB // GROUPS


def layer_kernel(
    query_hbm,
    cache_hbm,
    new_latent,
    lengths,
    vu_hbm,
    hidden,
    gain,
    counts,
    wo_hbm,
    wg_hbm,
    wu_hbm,
    wd_hbm,
    out,
    query,
    cache,
    vu,
    lat,
    lat_in,
    by_head,
    heads_out,
    heads,
    q_sem,
    c_sem,
    lat_sem,
    heads_sem,
    heads_x_sem,
    vz_sem,
    vcore_sem,
    wo_own,
    wo,
    wd_own,
    wd_in,
    wd,
    wg,
    wu,
    own_sem,
    w_sem,
    inner,
    inner_sem,
    hid,
    hid_sem,
    square,
    square_in,
    square_sem,
    total,
    result,
    result_in,
    result_sem,
    far,
    far_in,
    far_sem,
    gain_row,
    *scratch,
):
    net = Net()
    z, x = net.z, net.x
    home = net.zdev(0)
    send = Sender()
    sum_heads = SumZ(net, send, *scratch[0:3])
    sum_ffn = SumZ(net, send, *scratch[3:6])
    wo_group = Regroup(net, send, wo_own, wo, *scratch[6:9])
    wd_group = Regroup(net, send, wd_own, wd_in, *scratch[9:12])
    ag = scratch[12:]

    z_others = RS_ORDER[:-1]
    barrier = pltpu.get_barrier_semaphore()
    partners = [net.zdev(k) for k in z_others] + [net.xdev(o) for o in XO]
    partners += [net.ydev(o) for o in XO] + [net.sibling]
    for dev in partners:
        pl.semaphore_signal(barrier, inc=1, device_id=dev, device_id_type=MESH)

    loads = []
    for i in range(GROUPS):
        part = pl.ds(i * SIZE, SIZE)
        loads.append(
            (
                pltpu.make_async_copy(query_hbm.at[part], query.at[part], q_sem.at[i]),
                pltpu.make_async_copy(cache_hbm.at[part], cache.at[part], c_sem.at[i]),
            )
        )
    own_vu = pltpu.make_async_copy(vu_hbm, vu.at[z], own_sem.at[0])
    own_wo = pltpu.make_async_copy(
        wo_hbm.at[pl.ds(pl.multiple_of(net.g * 32, 32), 32)], wo_own, own_sem.at[1]
    )
    own_wd = pltpu.make_async_copy(
        wd_hbm.at[pl.ds(pl.multiple_of(net.y * 64 + net.core * 48, 16), 48)], wd_own, own_sem.at[2]
    )
    weights = []
    for i, (src, dst) in enumerate(((wg_hbm, wg), (wu_hbm, wu))):
        weights.append(pltpu.make_async_copy(src, dst.at[0:FD], w_sem.at[i, 0]))
        for j in range(1, FREP):
            weights.append(
                pltpu.make_async_copy(
                    src.at[FM:FD], dst.at[FM + j * FR : FM + (j + 1) * FR], w_sem.at[i, j]
                )
            )

    def begin(copies):
        for copy in copies:
            copy.start()

    begin([*loads[0], own_vu, own_wo, *loads[1]])

    gain_row[...] = gain[...].astype(F32).reshape(1, D)
    value_up = ValueUp(net, send, vu, vz_sem, vcore_sem)
    order = order_matrix(
        64, lambda i: ((i & 15) >> 1) * 8 + (i >> 4) * 2 + (i & 1)
    )
    lat_box = Inbox(send, lat_sem, home)
    hid_box = Inbox(send, hid_sem, home)
    later = ([*loads[2]], [*loads[3]], [own_wd], weights)
    for i in range(GROUPS):
        for copy in loads[i]:
            copy.wait()
        begin(later[i])
        attend(range(i * SIZE, (i + 1) * SIZE), query, cache, new_latent, lengths, order, lat)
        if i == 0:
            own_vu.wait()
            own_wo.wait()
            pl.semaphore_wait(barrier, len(partners))
            value_up.start(1)
            wo_group.start()
        part = pl.ds(i * SIZE, SIZE)
        for o in XO:
            lat_box.push(lat.at[net.xc(o), part], lat_in.at[o - 1, part], (o - 1, i), net.xdev(o))
        if i == 1:
            wo_group.spread()
            value_up.forward(1)
    for o in XO:
        hid_box.push(hidden.at[:, xcols(net.xc(o))], hid.at[x], (o - 1,), net.xdev(o))
    hid[x] = hidden[:, xcols(x)]
    value_up.forward(2)

    swap = order_matrix(256, lambda i: ((i & 15) << 4) + (i >> 4))

    def sort(o):
        rows = lat[x] if o == 0 else lat_in[o - 1]
        value = jnp.dot(swap, rows.reshape(RB * 16, KVL), preferred_element_type=F32)
        by_head[:, net.xc(-o)] = value.astype(BF16).reshape(16, RB, KVL)

    sort(0)
    value_up.forward(3)
    wo_group.pass_on()
    for o in XO:
        for i in range(GROUPS):
            lat_box.wait(lat_in.at[o - 1, pl.ds(i * SIZE, SIZE)], (o - 1, i))
        sort(o)
    own_wd.wait()
    wd_group.start()
    value_up.forward(4)
    value_up.finish()

    heads_box = Inbox(send, heads_sem, home)
    for i, k in enumerate(RS_ORDER):
        c = net.zc(k)
        for j in range(2):
            rows = by_head[c * 2 + j].reshape(ZB, KVL)
            value = jnp.dot(rows, vu[c, j], preferred_element_type=F32).astype(BF16)
            cols = slice(j * VHD, (j + 1) * VHD)
            if k:
                heads_out[c, :, cols] = value
            else:
                heads[z, x, :, cols] = value
        if k:
            heads_box.push(heads_out.at[c], heads.at[z, x], (i,), net.zdev(k))

    def heads_block(k, q):
        return heads.at[net.zc(k), q]

    heads_x = AlongX(net, send, heads_block, heads_x_sem)

    def project(k):
        c = net.zc(k)
        heads_x.finish(k)
        rows = jnp.concatenate([heads[c, q] for q in range(NX)], axis=1)
        term = jnp.dot(rows, wo[...].reshape(NX * 256, DX), preferred_element_type=F32)
        if k:
            sum_heads.step(k, term)
            return
        for o in XO:
            hid_box.wait(hid.at[net.xc(-o)], (o - 1,))
        for h in range(2):
            before = hid[2 * h : 2 * h + 2].reshape(ZB // 2, DX).astype(F32)
            total[half(h)] = before + (term[half(h)] + sum_heads.last(h))

    for i, k in enumerate(RS_ORDER):
        if k:
            heads_box.wait(heads.at[net.zc(k), x], (z_others.index(-k if k < 4 else 4),))
        heads_x.push(k)
    wo_group.finish()
    wd_group.spread()
    for k in RS_ORDER:
        project(k)

    rows = ag[0]
    residual = total[...]
    sums = jnp.sum(residual * residual, axis=-1, keepdims=True)
    lane = lax.broadcasted_iota(jnp.int32, (RB, FR * FREP), 1) // FR
    packed = jnp.broadcast_to(sums[0:RB], (RB, 128))
    for q in range(1, FREP):
        packed = jnp.where(lane == q, sums[q * RB : (q + 1) * RB], packed)
    square[...] = packed
    square_box = Inbox(send, square_sem, home)
    for o in XO:
        square_box.push(square, square_in.at[o - 1], (o - 1,), net.xdev(o))
    for o in XO:
        square_box.wait(square_in.at[o - 1], (o - 1,))
        packed = packed + square_in[o - 1]
    sums = jnp.concatenate([packed[:, q * FR : q * FR + 1] for q in range(FREP)], axis=0)
    mean_sq = sums * (1.0 / D)
    scaled = total[...] * lax.rsqrt(mean_sq + 1e-06) * gain_row[:, xcols(x)]
    rows[z, x] = scaled.astype(BF16)

    for copy in weights:
        copy.wait()

    def inner_block(k, q):
        return inner.at[net.zc(k), q]

    inner_x = AlongX(net, send, inner_block, inner_sem)

    def feed(ks):
        chunk = jnp.concatenate(
            [jnp.concatenate([rows[net.zc(k), q] for q in range(NX)], axis=1) for k in ks], axis=0
        )
        dims = (((1,), (1,)), ((), ()))
        gate = lax.dot_general(chunk, wg[...], dims, preferred_element_type=F32)
        up = lax.dot_general(chunk, wu[...], dims, preferred_element_type=F32)
        act = gate / (1.0 + jnp.exp(-gate)) * up
        for i, k in enumerate(ks):
            store(k, act[i * ZB : (i + 1) * ZB])

    def store(k, act):
        c = net.zc(k)
        for j in range(2):
            inner[c, x, j * ZB : (j + 1) * ZB] = act[:, j * 128 : (j + 1) * 128].astype(BF16)
        rest = act[:, FM:FK]
        packed = rest[0:RB]
        for q in range(1, FREP):
            packed = jnp.where(lane == q, rest[q * RB : (q + 1) * RB], packed)
        inner[c, x, 2 * ZB : 2 * ZB + RB] = packed.astype(BF16)
        inner_x.push(k)

    def between(stage):
        if stage == 0:
            wd_group.pass_on()
            return
        wd_group.finish()
        for q in range(NX):
            for g, low, count, to in (
                (0, 0, 48, 0),
                (1, 0, 48, 48),
                (2, 32, 16, 96),
                (3, 0, 48, 112),
                (4, 32, 16, 160),
                (5, 0, 48, 176),
                (6, 32, 16, 224),
                (7, 0, 16, 240),
            ):
                wd[q * FM + to : q * FM + to + count] = wd_in[q, g, low : low + count]
            for j in range(FREP):
                to = NX * FM + (q * FREP + j) * FR
                wd[to : to + FR] = wd_in[q, 7, 16 : 16 + FR]

    all_gather(net, send, feed, between, *ag)

    far_box = Inbox(send, far_sem, home)
    group = lax.broadcasted_iota(jnp.int32, (ZB, FR * FREP), 1) // FR
    mine = group == lax.broadcasted_iota(jnp.int32, (ZB, FR * FREP), 0) // RB
    for k in (-3, 3, 4, -2, 2, -1, 1, 0):
        c = net.zc(k)
        inner_x.finish(k)
        columns = []
        for q in range(NX):
            columns += [inner[c, q, 0:ZB], inner[c, q, ZB : 2 * ZB]]
        for q in range(NX):
            rest = jnp.concatenate([inner[c, q, 2 * ZB : 2 * ZB + RB]] * FREP, axis=0)
            columns.append(jnp.where(mine, rest, jnp.zeros_like(rest)))
        term = jnp.dot(jnp.concatenate(columns, axis=1), wd[...], preferred_element_type=F32)
        if k == 4:
            far[...] = term.astype(BF16)
            far_box.push(far, far_in, (), net.zdev(4))
            continue
        if k:
            sum_ffn.step(k, term, chained=False)
            continue
        far_box.wait(far_in, ())
        term = term + far_in[...].astype(F32)
        for h in range(2):
            value = total[half(h)] + (term[half(h)] + sum_ffn.last(h))
            result[2 * h : 2 * h + 2] = value.astype(BF16).reshape(2, RB, DX)

    result_box = Inbox(send, result_sem, home)
    for o in XO:
        result_box.push(result.at[net.xc(o)], result_in.at[x], (o - 1,), net.xdev(o))
    result_in[x] = result[x]
    for o in XO:
        result_box.wait(result_in.at[net.xc(-o)], (o - 1,))
    live = lax.broadcasted_iota(jnp.int32, (RB, DX), 0) < counts[0]
    for q in range(NX):
        value = result_in[q]
        out[:, xcols(q)] = jnp.where(live, value, jnp.zeros_like(value))
    send.finish()


def per_device(
    query,
    cache,
    new_latent,
    lengths,
    counts,
    hidden_in,
    value_up,
    out_proj,
    norm_gain,
    w_gate,
    w_up,
    w_down,
):
    cache = cache.transpose(0, 2, 1)
    w_gate, w_up = w_gate.T, w_up.T
    vmem = pl.BlockSpec(memory_space=pltpu.VMEM)
    smem = pl.BlockSpec(memory_space=pltpu.SMEM)
    hbm = pl.BlockSpec(memory_space=pl.ANY)
    dma = pltpu.SemaphoreType.DMA
    return pl.pallas_call(
        layer_kernel,
        out_shape=jax.ShapeDtypeStruct((RB, D), BF16),
        in_specs=[hbm, hbm, vmem, smem, hbm, vmem, vmem, smem, hbm, hbm, hbm, hbm],
        out_specs=vmem,
        scratch_shapes=[
            pltpu.VMEM(query.shape, BF16),
            pltpu.VMEM(cache.shape, BF16),
            pltpu.VMEM((NZ, 2, KVL, VHD), BF16),
            pltpu.VMEM((NX, RB, 16, KVL), BF16),
            pltpu.VMEM((3, RB, 16, KVL), BF16),
            pltpu.VMEM((16, NX, RB, KVL), BF16),
            pltpu.VMEM((NZ, ZB, 2 * VHD), BF16),
            pltpu.VMEM((NZ, NX, ZB, 2 * VHD), BF16),
            dma((GROUPS,)),
            dma((GROUPS,)),
            dma((2, 3, GROUPS)),
            dma((2, 7)),
            ALONG_X_SEM,
            dma((2, 2, 4)),
            dma((2, 2, 4)),
            pltpu.VMEM((32, D), BF16),
            pltpu.VMEM((NX, 8, 32, DX), BF16),
            pltpu.VMEM((48, D), BF16),
            pltpu.VMEM((NX, 8, 48, DX), BF16),
            pltpu.VMEM((NX * FK, DX), BF16),
            pltpu.VMEM((FK, D), BF16),
            pltpu.VMEM((FK, D), BF16),
            dma((3,)),
            dma((2, FREP)),
            pltpu.VMEM((NZ, NX, 2 * ZB + RB, 128), BF16),
            ALONG_X_SEM,
            pltpu.VMEM((NX, RB, DX), BF16),
            dma((2, 3)),
            pltpu.VMEM((RB, 128), F32),
            pltpu.VMEM((3, RB, 128), F32),
            dma((2, 3)),
            pltpu.VMEM((ZB, DX), F32),
            pltpu.VMEM((NX, RB, DX), BF16),
            pltpu.VMEM((NX, RB, DX), BF16),
            dma((2, 3)),
            pltpu.VMEM((ZB, DX), BF16),
            pltpu.VMEM((ZB, DX), BF16),
            dma((2,)),
            pltpu.VMEM((1, D), F32),
            *SUM_SCRATCH,
            *SUM_SCRATCH,
            *REGROUP_SEMS,
            *REGROUP_SEMS,
            *AG_SCRATCH,
        ],
        compiler_params=pltpu.CompilerParams(
            collective_id=1, has_side_effects=True, vmem_limit_bytes=60 << 20
        ),
        name="layer",
    )(
        query,
        cache,
        new_latent,
        lengths,
        value_up,
        hidden_in,
        norm_gain,
        counts,
        out_proj,
        w_gate,
        w_up,
        w_down,
    )


def solution(mesh):
    return jax.shard_map(
        per_device,
        mesh=mesh,
        in_specs=(
            P(("grp", "dp"), None, None),
            P(("grp", "dp"), None, None),
            P(("grp", "dp"), None),
            P(("grp", "dp")),
            P(("grp", "dp")),
            P(("grp", "dp"), None),
            P("dp", None, None),
            P("dp", None),
            P(),
            P(None, "dp"),
            P(None, "dp"),
            P("dp", None),
        ),
        out_specs=P(("grp", "dp"), None),
        check_vma=False,
    )
```

```python
import jax
import jax.numpy as jnp
from jax import lax
from jax.experimental import pallas as pl
from jax.experimental.pallas import tpu as pltpu
from jax.sharding import PartitionSpec as P

score_scale = 192.0 ** (-0.5)
MESH = pl.DeviceIdType.MESH
F32 = jnp.float32
BF16 = jnp.bfloat16

NZ, NX, NY = 8, 4, 4
RB = 16
ZB = NX * RB
D = 3584
DX = D // NX
KVL = 512
VHD = 128
CTX = 256
FD = 288
FM, FR, FREP = 256, 32, 4
FK = FM + FR * FREP
CA = 384
PLUS, MINUS = 0, 1
STEP = (1, -1)
XO = (1, 3, 2)
RS_ORDER = (4, -3, 3, -2, 2, -1, 1, 0)


def half(h):
    return slice(h * ZB // 2, (h + 1) * ZB // 2)


class Net:
    def __init__(self):
        self.g = lax.axis_index("grp")
        self.d = lax.axis_index("dp")
        self.z = self.d // NX
        self.x = lax.rem(self.d, NX)
        self.y = self.g // 2
        self.core = lax.rem(self.g, 2)
        self.sibling = (self.g + 1 - 2 * self.core, self.d)

    def zc(self, k):
        return lax.rem(self.z + (k + NZ), NZ)

    def xc(self, k):
        return lax.rem(self.x + (k + NX), NX)

    def yc(self, k):
        return lax.rem(self.y + (k + NY), NY)

    def zdev(self, k):
        return (self.g, self.zc(k) * NX + self.x)

    def xdev(self, k):
        return (self.g, self.z * NX + self.xc(k))

    def ydev(self, k):
        return (self.yc(k) * 2 + self.core, self.d)


def xcols(q):
    if isinstance(q, int):
        return slice(q * DX, (q + 1) * DX)
    return pl.ds(pl.multiple_of(q * DX, 128), DX)


class Sender:
    def __init__(self):
        self.started = []

    def start(self, src, dst, ssem, rsem, dev):
        copy = pltpu.make_async_remote_copy(
            src_ref=src,
            dst_ref=dst,
            send_sem=ssem,
            recv_sem=rsem,
            device_id=dev,
            device_id_type=MESH,
        )
        copy.start()
        self.started.append(copy)

    def finish(self):
        for copy in self.started:
            copy.wait_send()


def wait_recv(dst, ssem, rsem, dev):
    pltpu.make_async_remote_copy(
        src_ref=dst,
        dst_ref=dst,
        send_sem=ssem,
        recv_sem=rsem,
        device_id=dev,
        device_id_type=MESH,
    ).wait_recv()


class Inbox:
    def __init__(self, send, sems, home):
        self.send, self.sems, self.home = send, sems, home

    def push(self, src, dst, index, dev):
        self.send.start(src, dst, self.sems.at[(0, *index)], self.sems.at[(1, *index)], dev)

    def wait(self, dst, index):
        wait_recv(dst, self.sems.at[(0, *index)], self.sems.at[(1, *index)], self.home)


class AlongX:
    def __init__(self, net, send, block, sem):
        self.net, self.block = net, block
        self.box = Inbox(send, sem, net.zdev(0))

    def push(self, k):
        ref = self.block(k, self.net.x)
        for o in XO:
            self.box.push(ref, ref, (o - 1, RS_ORDER.index(k)), self.net.xdev(o))

    def finish(self, k):
        for o in XO:
            self.box.wait(self.block(k, self.net.xc(-o)), (o - 1, RS_ORDER.index(k)))


ALONG_X_SEM = pltpu.SemaphoreType.DMA((2, 3, NZ))


class Regroup:
    def __init__(self, net, send, own, buf, x_sem, y_sem, core_sem):
        self.net, self.own, self.buf = net, own, buf
        home = net.zdev(0)
        self.over_x = Inbox(send, x_sem, home)
        self.over_y = Inbox(send, y_sem, home)
        self.across = Inbox(send, core_sem, home)

    def start(self):
        net = self.net
        for o in XO:
            src = self.own.at[:, xcols(net.xc(o))]
            self.over_x.push(src, self.buf.at[net.x, net.g], (o - 1,), net.xdev(o))
        self.buf[net.x, net.g] = self.own[:, xcols(net.x)]

    def spread(self):
        net = self.net
        for o in XO:
            self.over_x.wait(self.buf.at[net.xc(-o), net.g], (o - 1,))
        ref = self.buf.at[:, net.g]
        for o in XO:
            self.over_y.push(ref, ref, (o - 1,), net.ydev(o))
        self.across.push(ref, ref, (0,), net.sibling)

    def pass_on(self):
        net = self.net
        for o in XO:
            ref = self.buf.at[:, net.yc(-o) * 2 + net.core]
            self.over_y.wait(ref, (o - 1,))
            self.across.push(ref, ref, (o,), net.sibling)

    def finish(self):
        net = self.net
        for o in range(NY):
            self.across.wait(self.buf.at[:, net.yc(-o) * 2 + 1 - net.core], (o,))


REGROUP_SEMS = [
    pltpu.SemaphoreType.DMA((2, 3)),
    pltpu.SemaphoreType.DMA((2, 3)),
    pltpu.SemaphoreType.DMA((2, 4)),
]

SUM_SCRATCH = [
    pltpu.VMEM((NZ, ZB, DX), BF16),
    pltpu.VMEM((2, 4, 2, ZB // 2, DX), BF16),
    pltpu.SemaphoreType.DMA((2, 2, 4, 2)),
]


class SumZ:
    def __init__(self, net, send, part, came, sem):
        self.net, self.part, self.came = net, part, came
        self.box = Inbox(send, sem, net.zdev(0))

    def step(self, k, term, chained=True):
        c = self.net.zc(k)
        d = PLUS if k > 0 else MINUS
        for h in (0, 1) if k == 4 else (1 - d, d):
            value = term[half(h)]
            hops = abs(k)
            if k == 4:
                d = h
            elif hops < 3 or (chained and h == d):
                self.box.wait(self.came.at[d, hops, h], (d, hops, h))
                value = value + self.came[d, hops, h].astype(F32)
            self.part[c, half(h)] = value.astype(BF16)
            self.box.push(
                self.part.at[c, half(h)],
                self.came.at[d, hops - 1, h],
                (d, hops - 1, h),
                self.net.zdev(STEP[d]),
            )

    def last(self, h):
        for d in (PLUS, MINUS):
            self.box.wait(self.came.at[d, 0, h], (d, 0, h))
        return self.came[PLUS, 0, h].astype(F32) + self.came[MINUS, 0, h].astype(F32)


AG_SCRATCH = [
    pltpu.VMEM((NZ, NX, ZB, DX), BF16),
    ALONG_X_SEM,
    pltpu.SemaphoreType.DMA((2, 2, 4)),
    pltpu.SemaphoreType.DMA((2, 2, 4, 2)),
    pltpu.SemaphoreType.DMA((2, 3)),
]


def all_gather(net, send, use, between, rows, ax_sem, az_sem, bz_sem, bx_sem):
    z, x = net.z, net.x
    home = net.zdev(0)
    az, bz, bx = (Inbox(send, sem, home) for sem in (az_sem, bz_sem, bx_sem))

    def a_block(k, q):
        return rows.at[net.zc(k), q, :, 0:CA]

    ax = AlongX(net, send, a_block, ax_sem)

    def a_ref(k, hops, d):
        return rows.at[net.zc(k), x, slice(0, ZB) if hops < 4 else half(d), 0:CA]

    def a_send(hops, d):
        ref = a_ref(-STEP[d] * (hops - 1), hops, d)
        az.push(ref, ref, (d, hops - 1), net.zdev(STEP[d]))

    def b_ref(k, h):
        return rows.at[net.zc(k), :, half(h), CA:DX]

    def b_send(hops, d, h):
        ref = b_ref(-STEP[d] * (hops - 1), h)
        bz.push(ref, ref, (d, hops - 1, h), net.zdev(STEP[d]))

    def step_a(hops):
        for d in (PLUS, MINUS):
            az.wait(a_ref(-STEP[d] * hops, hops, d), (d, hops - 1))
            if hops < 4:
                a_send(hops + 1, d)
                ax.push(-STEP[d] * hops)
        if hops == 4:
            ax.push(4)

    def step_b(hops, far):
        for d in (PLUS, MINUS):
            h = d if far else 1 - d
            bz.wait(b_ref(-STEP[d] * hops, h), (d, hops - 1, h))
            if hops < 3 or (hops == 3 and far):
                b_send(hops + 1, d, h)

    def finish(*ks):
        for k in ks:
            ax.finish(k)
        use(ks)

    for d in (PLUS, MINUS):
        a_send(1, d)
    own_b = rows.at[z, x, :, CA:DX]
    for o in XO:
        bx.push(own_b, own_b, (o - 1,), net.xdev(o))
    ax.push(0)
    step_a(1)
    for o in XO:
        bx.wait(rows.at[z, net.xc(-o), :, CA:DX], (o - 1,))
    for far in (True, False):
        for d in (PLUS, MINUS):
            b_send(1, d, d if far else 1 - d)
    step_a(2)
    finish(0)
    step_b(1, True)
    step_a(3)
    step_b(1, False)
    step_a(4)
    finish(-1, 1)
    step_b(2, True)
    step_b(2, False)
    finish(-2, 2)
    step_b(3, True)
    step_b(3, False)
    between(0)
    finish(-3, 3)
    step_b(4, True)
    between(1)
    finish(4)


class ValueUp:
    def __init__(self, net, send, vu, z_sem, core_sem):
        self.net, self.vu = net, vu
        self.core, self.other = net.core, net.sibling
        home = net.zdev(0)
        self.along = Inbox(send, z_sem, home)
        self.across = Inbox(send, core_sem, home)

    def ref(self, k, hops, d, head):
        rows = slice(0, KVL) if hops < 4 else slice(d * (KVL // 2), (d + 1) * (KVL // 2))
        return self.vu.at[self.net.zc(k), head, rows]

    def start(self, hops):
        for d, step in ((PLUS, 1), (MINUS, -1)):
            ref = self.ref(-step * (hops - 1), hops, d, self.core)
            self.along.push(ref, ref, (d, hops - 1), self.net.zdev(step))

    def forward(self, hops):
        for d, step in ((PLUS, 1), (MINUS, -1)):
            ref = self.ref(-step * hops, hops, d, self.core)
            self.along.wait(ref, (d, hops - 1))
            self.across.push(ref, ref, (d, hops - 1), self.other)
        if hops < 4:
            self.start(hops + 1)

    def finish(self):
        for hops in range(1, 5):
            for d, step in ((PLUS, 1), (MINUS, -1)):
                self.across.wait(self.ref(-step * hops, hops, d, 1 - self.core), (d, hops - 1))


def order_matrix(n, source):
    i = lax.broadcasted_iota(jnp.int32, (n, n), 0)
    j = lax.broadcasted_iota(jnp.int32, (n, n), 1)
    return jnp.where(source(i) == j, 1.0, 0.0).astype(BF16)


def attend(rs, query, cache, new_latent, lengths, order, lat):
    qs = [query[r] for r in rs]
    scores = [jnp.dot(q, cache[r], preferred_element_type=F32) * score_scale for q, r in zip(qs, rs)]
    news = [new_latent[r : r + 1, :].astype(F32) for r in rs]
    own = [
        jnp.sum(q.astype(F32) * new, axis=-1, keepdims=True) * score_scale
        for q, new in zip(qs, news)
    ]
    position = lax.broadcasted_iota(jnp.int32, (1, CTX), 1)
    scores = [jnp.where(position < lengths[r], s, -jnp.inf) for s, r in zip(scores, rs)]
    tops = [jnp.maximum(jnp.max(s, axis=-1, keepdims=True), o) for s, o in zip(scores, own)]
    weights = [jnp.exp(s - top) for s, top in zip(scores, tops)]
    own = [jnp.exp(o - top) for o, top in zip(own, tops)]
    sums = [jnp.sum(w, axis=-1, keepdims=True) + o for w, o in zip(weights, own)]
    mixed = [
        lax.dot_general(
            w.astype(BF16),
            cache[r, 0:KVL, :],
            (((1,), (1,)), ((), ())),
            preferred_element_type=F32,
        )
        for w, r in zip(weights, rs)
    ]
    latent = [
        ((m + o.astype(BF16).astype(F32) * new[:, 0:KVL]) * (1.0 / s)).astype(BF16)
        for m, o, new, s in zip(mixed, own, news, sums)
    ]
    latent = [jnp.dot(order, value, preferred_element_type=F32).astype(BF16) for value in latent]
    for value, r in zip(latent, rs):
        for to in range(NX):
            lat[to, r] = value[to * 16 : (to + 1) * 16]


GROUPS = 4
SIZE = RB // GROUPS


def layer_kernel(
    query_hbm,
    cache_hbm,
    new_latent,
    lengths,
    vu_hbm,
    hidden,
    gain,
    counts,
    wo_hbm,
    wg_hbm,
    wu_hbm,
    wd_hbm,
    out,
    query,
    cache,
    vu,
    lat,
    lat_in,
    by_head,
    heads_out,
    heads,
    q_sem,
    c_sem,
    lat_sem,
    heads_sem,
    heads_x_sem,
    vz_sem,
    vcore_sem,
    wo_own,
    wo,
    wd_own,
    wd_in,
    wd,
    wg,
    wu,
    own_sem,
    w_sem,
    inner,
    inner_sem,
    hid,
    hid_sem,
    square,
    square_in,
    square_sem,
    total,
    result,
    result_in,
    result_sem,
    far,
    far_in,
    far_sem,
    gain_row,
    *scratch,
):
    net = Net()
    z, x = net.z, net.x
    home = net.zdev(0)
    send = Sender()
    sum_heads = SumZ(net, send, *scratch[0:3])
    sum_ffn = SumZ(net, send, *scratch[3:6])
    wo_group = Regroup(net, send, wo_own, wo, *scratch[6:9])
    wd_group = Regroup(net, send, wd_own, wd_in, *scratch[9:12])
    ag = scratch[12:]

    z_others = RS_ORDER[:-1]
    barrier = pltpu.get_barrier_semaphore()
    partners = [net.zdev(k) for k in z_others] + [net.xdev(o) for o in XO]
    partners += [net.ydev(o) for o in XO] + [net.sibling]
    for dev in partners:
        pl.semaphore_signal(barrier, inc=1, device_id=dev, device_id_type=MESH)

    loads = []
    for i in range(GROUPS):
        part = pl.ds(i * SIZE, SIZE)
        loads.append(
            (
                pltpu.make_async_copy(query_hbm.at[part], query.at[part], q_sem.at[i]),
                pltpu.make_async_copy(cache_hbm.at[part], cache.at[part], c_sem.at[i]),
            )
        )
    own_vu = pltpu.make_async_copy(vu_hbm, vu.at[z], own_sem.at[0])
    own_wo = pltpu.make_async_copy(
        wo_hbm.at[pl.ds(pl.multiple_of(net.g * 32, 32), 32)], wo_own, own_sem.at[1]
    )
    own_wd = pltpu.make_async_copy(
        wd_hbm.at[pl.ds(pl.multiple_of(net.y * 64 + net.core * 48, 16), 48)], wd_own, own_sem.at[2]
    )
    weights = []
    for i, (src, dst) in enumerate(((wg_hbm, wg), (wu_hbm, wu))):
        weights.append(pltpu.make_async_copy(src, dst.at[0:FD], w_sem.at[i, 0]))
        for j in range(1, FREP):
            weights.append(
                pltpu.make_async_copy(
                    src.at[FM:FD], dst.at[FM + j * FR : FM + (j + 1) * FR], w_sem.at[i, j]
                )
            )

    def begin(copies):
        for copy in copies:
            copy.start()

    begin([*loads[0], own_vu, own_wo, *loads[1]])

    gain_row[...] = gain[...].astype(F32).reshape(1, D)
    value_up = ValueUp(net, send, vu, vz_sem, vcore_sem)
    order = order_matrix(
        64, lambda i: ((i & 15) >> 1) * 8 + (i >> 4) * 2 + (i & 1)
    )
    lat_box = Inbox(send, lat_sem, home)
    hid_box = Inbox(send, hid_sem, home)
    later = ([*loads[2]], [*loads[3]], [own_wd], weights)
    for i in range(GROUPS):
        for copy in loads[i]:
            copy.wait()
        begin(later[i])
        attend(range(i * SIZE, (i + 1) * SIZE), query, cache, new_latent, lengths, order, lat)
        if i == 0:
            own_vu.wait()
            own_wo.wait()
            pl.semaphore_wait(barrier, len(partners))
            value_up.start(1)
            wo_group.start()
        part = pl.ds(i * SIZE, SIZE)
        for o in XO:
            lat_box.push(lat.at[net.xc(o), part], lat_in.at[o - 1, part], (o - 1, i), net.xdev(o))
        if i == 1:
            wo_group.spread()
            value_up.forward(1)
    for o in XO:
        hid_box.push(hidden.at[:, xcols(net.xc(o))], hid.at[x], (o - 1,), net.xdev(o))
    hid[x] = hidden[:, xcols(x)]
    value_up.forward(2)

    swap = order_matrix(256, lambda i: ((i & 15) << 4) + (i >> 4))

    def sort(o):
        rows = lat[x] if o == 0 else lat_in[o - 1]
        value = jnp.dot(swap, rows.reshape(RB * 16, KVL), preferred_element_type=F32)
        by_head[:, net.xc(-o)] = value.astype(BF16).reshape(16, RB, KVL)

    sort(0)
    value_up.forward(3)
    wo_group.pass_on()
    for o in XO:
        for i in range(GROUPS):
            lat_box.wait(lat_in.at[o - 1, pl.ds(i * SIZE, SIZE)], (o - 1, i))
        sort(o)
    own_wd.wait()
    wd_group.start()
    value_up.forward(4)
    value_up.finish()

    heads_box = Inbox(send, heads_sem, home)
    for i, k in enumerate(RS_ORDER):
        c = net.zc(k)
        for j in range(2):
            rows = by_head[c * 2 + j].reshape(ZB, KVL)
            value = jnp.dot(rows, vu[c, j], preferred_element_type=F32).astype(BF16)
            cols = slice(j * VHD, (j + 1) * VHD)
            if k:
                heads_out[c, :, cols] = value
            else:
                heads[z, x, :, cols] = value
        if k:
            heads_box.push(heads_out.at[c], heads.at[z, x], (i,), net.zdev(k))

    def heads_block(k, q):
        return heads.at[net.zc(k), q]

    heads_x = AlongX(net, send, heads_block, heads_x_sem)

    def project(ks):
        for k in ks:
            heads_x.finish(k)
        rows = jnp.concatenate(
            [jnp.concatenate([heads[net.zc(k), q] for q in range(NX)], axis=1) for k in ks], axis=0
        )
        terms = jnp.dot(rows, wo[...].reshape(NX * 256, DX), preferred_element_type=F32)
        for i, k in enumerate(ks):
            add_heads(k, terms[i * ZB : (i + 1) * ZB])

    def add_heads(k, term):
        if k:
            sum_heads.step(k, term)
            return
        for o in XO:
            hid_box.wait(hid.at[net.xc(-o)], (o - 1,))
        for h in range(2):
            before = hid[2 * h : 2 * h + 2].reshape(ZB // 2, DX).astype(F32)
            total[half(h)] = before + (term[half(h)] + sum_heads.last(h))

    for i, k in enumerate(RS_ORDER):
        if k:
            heads_box.wait(heads.at[net.zc(k), x], (z_others.index(-k if k < 4 else 4),))
        heads_x.push(k)
    wo_group.finish()
    wd_group.spread()
    for ks in ((4,), (-3, 3), (-2, 2), (-1, 1), (0,)):
        project(ks)

    rows = ag[0]
    residual = total[...]
    sums = jnp.sum(residual * residual, axis=-1, keepdims=True)
    lane = lax.broadcasted_iota(jnp.int32, (RB, FR * FREP), 1) // FR
    packed = jnp.broadcast_to(sums[0:RB], (RB, 128))
    for q in range(1, FREP):
        packed = jnp.where(lane == q, sums[q * RB : (q + 1) * RB], packed)
    square[...] = packed
    square_box = Inbox(send, square_sem, home)
    for o in XO:
        square_box.push(square, square_in.at[o - 1], (o - 1,), net.xdev(o))
    for o in XO:
        square_box.wait(square_in.at[o - 1], (o - 1,))
        packed = packed + square_in[o - 1]
    sums = jnp.concatenate([packed[:, q * FR : q * FR + 1] for q in range(FREP)], axis=0)
    mean_sq = sums * (1.0 / D)
    scaled = total[...] * lax.rsqrt(mean_sq + 1e-06) * gain_row[:, xcols(x)]
    rows[z, x] = scaled.astype(BF16)

    for copy in weights:
        copy.wait()

    def inner_block(k, q):
        return inner.at[net.zc(k), q]

    inner_x = AlongX(net, send, inner_block, inner_sem)

    def feed(ks):
        chunk = jnp.concatenate(
            [jnp.concatenate([rows[net.zc(k), q] for q in range(NX)], axis=1) for k in ks], axis=0
        )
        dims = (((1,), (1,)), ((), ()))
        gate = lax.dot_general(chunk, wg[...], dims, preferred_element_type=F32)
        up = lax.dot_general(chunk, wu[...], dims, preferred_element_type=F32)
        act = gate / (1.0 + jnp.exp(-gate)) * up
        for i, k in enumerate(ks):
            store(k, act[i * ZB : (i + 1) * ZB])

    def store(k, act):
        c = net.zc(k)
        for j in range(2):
            inner[c, x, j * ZB : (j + 1) * ZB] = act[:, j * 128 : (j + 1) * 128].astype(BF16)
        rest = act[:, FM:FK]
        packed = rest[0:RB]
        for q in range(1, FREP):
            packed = jnp.where(lane == q, rest[q * RB : (q + 1) * RB], packed)
        inner[c, x, 2 * ZB : 2 * ZB + RB] = packed.astype(BF16)
        inner_x.push(k)

    def between(stage):
        if stage == 0:
            wd_group.pass_on()
            return
        wd_group.finish()
        for q in range(NX):
            for g, low, count, to in (
                (0, 0, 48, 0),
                (1, 0, 48, 48),
                (2, 32, 16, 96),
                (3, 0, 48, 112),
                (4, 32, 16, 160),
                (5, 0, 48, 176),
                (6, 32, 16, 224),
                (7, 0, 16, 240),
            ):
                wd[q * FM + to : q * FM + to + count] = wd_in[q, g, low : low + count]
            for j in range(FREP):
                to = NX * FM + (q * FREP + j) * FR
                wd[to : to + FR] = wd_in[q, 7, 16 : 16 + FR]

    all_gather(net, send, feed, between, *ag)

    far_box = Inbox(send, far_sem, home)
    group = lax.broadcasted_iota(jnp.int32, (ZB, FR * FREP), 1) // FR
    mine = group == lax.broadcasted_iota(jnp.int32, (ZB, FR * FREP), 0) // RB

    def inner_rows(k):
        c = net.zc(k)
        columns = []
        for q in range(NX):
            columns += [inner[c, q, 0:ZB], inner[c, q, ZB : 2 * ZB]]
        for q in range(NX):
            rest = jnp.concatenate([inner[c, q, 2 * ZB : 2 * ZB + RB]] * FREP, axis=0)
            columns.append(jnp.where(mine, rest, jnp.zeros_like(rest)))
        return jnp.concatenate(columns, axis=1)

    def add_ffn(k, term):
        if k == 4:
            far[...] = term.astype(BF16)
            far_box.push(far, far_in, (), net.zdev(4))
            return
        if k:
            sum_ffn.step(k, term, chained=False)
            return
        far_box.wait(far_in, ())
        term = term + far_in[...].astype(F32)
        for h in range(2):
            value = total[half(h)] + (term[half(h)] + sum_ffn.last(h))
            result[2 * h : 2 * h + 2] = value.astype(BF16).reshape(2, RB, DX)

    for ks in ((-3, 3), (4,), (-2, 2), (-1, 1), (0,)):
        for k in ks:
            inner_x.finish(k)
        rows_in = jnp.concatenate([inner_rows(k) for k in ks], axis=0)
        terms = jnp.dot(rows_in, wd[...], preferred_element_type=F32)
        for i, k in enumerate(ks):
            add_ffn(k, terms[i * ZB : (i + 1) * ZB])

    result_box = Inbox(send, result_sem, home)
    for o in XO:
        result_box.push(result.at[net.xc(o)], result_in.at[x], (o - 1,), net.xdev(o))
    result_in[x] = result[x]
    for o in XO:
        result_box.wait(result_in.at[net.xc(-o)], (o - 1,))
    live = lax.broadcasted_iota(jnp.int32, (RB, DX), 0) < counts[0]
    for q in range(NX):
        value = result_in[q]
        out[:, xcols(q)] = jnp.where(live, value, jnp.zeros_like(value))
    send.finish()


def per_device(
    query,
    cache,
    new_latent,
    lengths,
    counts,
    hidden_in,
    value_up,
    out_proj,
    norm_gain,
    w_gate,
    w_up,
    w_down,
):
    cache = cache.transpose(0, 2, 1)
    w_gate, w_up = w_gate.T, w_up.T
    vmem = pl.BlockSpec(memory_space=pltpu.VMEM)
    smem = pl.BlockSpec(memory_space=pltpu.SMEM)
    hbm = pl.BlockSpec(memory_space=pl.ANY)
    dma = pltpu.SemaphoreType.DMA
    return pl.pallas_call(
        layer_kernel,
        out_shape=jax.ShapeDtypeStruct((RB, D), BF16),
        in_specs=[hbm, hbm, vmem, smem, hbm, vmem, vmem, smem, hbm, hbm, hbm, hbm],
        out_specs=vmem,
        scratch_shapes=[
            pltpu.VMEM(query.shape, BF16),
            pltpu.VMEM(cache.shape, BF16),
            pltpu.VMEM((NZ, 2, KVL, VHD), BF16),
            pltpu.VMEM((NX, RB, 16, KVL), BF16),
            pltpu.VMEM((3, RB, 16, KVL), BF16),
            pltpu.VMEM((16, NX, RB, KVL), BF16),
            pltpu.VMEM((NZ, ZB, 2 * VHD), BF16),
            pltpu.VMEM((NZ, NX, ZB, 2 * VHD), BF16),
            dma((GROUPS,)),
            dma((GROUPS,)),
            dma((2, 3, GROUPS)),
            dma((2, 7)),
            ALONG_X_SEM,
            dma((2, 2, 4)),
            dma((2, 2, 4)),
            pltpu.VMEM((32, D), BF16),
            pltpu.VMEM((NX, 8, 32, DX), BF16),
            pltpu.VMEM((48, D), BF16),
            pltpu.VMEM((NX, 8, 48, DX), BF16),
            pltpu.VMEM((NX * FK, DX), BF16),
            pltpu.VMEM((FK, D), BF16),
            pltpu.VMEM((FK, D), BF16),
            dma((3,)),
            dma((2, FREP)),
            pltpu.VMEM((NZ, NX, 2 * ZB + RB, 128), BF16),
            ALONG_X_SEM,
            pltpu.VMEM((NX, RB, DX), BF16),
            dma((2, 3)),
            pltpu.VMEM((RB, 128), F32),
            pltpu.VMEM((3, RB, 128), F32),
            dma((2, 3)),
            pltpu.VMEM((ZB, DX), F32),
            pltpu.VMEM((NX, RB, DX), BF16),
            pltpu.VMEM((NX, RB, DX), BF16),
            dma((2, 3)),
            pltpu.VMEM((ZB, DX), BF16),
            pltpu.VMEM((ZB, DX), BF16),
            dma((2,)),
            pltpu.VMEM((1, D), F32),
            *SUM_SCRATCH,
            *SUM_SCRATCH,
            *REGROUP_SEMS,
            *REGROUP_SEMS,
            *AG_SCRATCH,
        ],
        compiler_params=pltpu.CompilerParams(
            collective_id=1, has_side_effects=True, vmem_limit_bytes=60 << 20
        ),
        name="layer",
    )(
        query,
        cache,
        new_latent,
        lengths,
        value_up,
        hidden_in,
        norm_gain,
        counts,
        out_proj,
        w_gate,
        w_up,
        w_down,
    )


def solution(mesh):
    return jax.shard_map(
        per_device,
        mesh=mesh,
        in_specs=(
            P(("grp", "dp"), None, None),
            P(("grp", "dp"), None, None),
            P(("grp", "dp"), None),
            P(("grp", "dp")),
            P(("grp", "dp")),
            P(("grp", "dp"), None),
            P("dp", None, None),
            P("dp", None),
            P(),
            P(None, "dp"),
            P(None, "dp"),
            P("dp", None),
        ),
        out_specs=P(("grp", "dp"), None),
        check_vma=False,
    )
```
